128 devices in a mesh: tm: 16 (over x, y), space: 8 (over z, core).
Axes of the slice: x: 4, y: 4, z: 4, core: 2. Of those that a mesh axis runs over, the one named last changes fastest.
Arguments:
- trajectory: float32 [64, 512, 1024], P('tm', 'space'), may hold values from -1.2 to 1.2
- initial_state: float32 [512, 1024], P('space'), may hold values from -1 to 1
- residual: float32 [64, 512, 1024], P('tm', 'space'), may hold values from -3000 to 3000
- mobility: float32 [512, 1024], P('space'), may hold values from 20 to 200
Outputs:
- update: float32 [64, 512, 1024], P('tm', 'space')
- reduction: float32 [], replicated
The draws below stay inside these ranges and needn't reach their ends.
All inputs are finite; a program needn't handle non-finite values.
Results may differ from the reference program's by a relative error of at most 0.00015.
Values sent between devices are 32-bit elements; how exact they have to be, the bound alone decides.
No kernel may reach another device: no remote copies, remote signals or barrier semaphores. Data moves between devices by JAX's collectives and lax.ppermute only.
A program may use at most 64 MiB of HBM per device.

```python
import math
import jax
import jax.numpy as jnp
from jax import lax

NT = 64
NCOL = 1024
SWEEPS = 16
NROWS = 512


def draw_residual(key, part):
    step_pos = jnp.arange(NT).astype(jnp.float32) / (NT - 1)
    row_pos = jnp.arange(NROWS).astype(jnp.float32) / (NROWS - 1)
    envelope = 40.0 * (1.0 + 2.0 * step_pos)[:, None, None] * (1.0 + 2.0 * row_pos)[None, :, None]
    samples = jnp.clip(jax.random.normal(key, (NT, NROWS, NCOL), jnp.float32), -5.0, 5.0)
    return (envelope * samples).astype(jnp.float32)


def block_levels(rng, shape, shards, least, high):
    def one(position, shards_of):
        heights = jax.random.uniform(jax.random.fold_in(jax.random.fold_in(rng, 6), position), (shards_of,), jnp.float32, least / len(shards), high / len(shards))
        return jnp.repeat(jnp.exp(heights), shape[position] // shards_of).reshape((-1,) + (1,) * (len(shape) - position - 1))

    level = one(*shards[0])
    for cut in shards[1:]:
        level = level * one(*cut)
    return level


def setup_inputs(seed: int = 0) -> dict:
    seeds = jax.random.split(jax.random.key(seed), 5)
    return {
        "trajectory": jnp.clip(jax.random.uniform(seeds[0], (NT, NROWS, NCOL), jnp.float32, -1.2, 1.2) * block_levels(seeds[0], (NT, NROWS, NCOL), ((0, 16), (1, 8)), -0.4, 0.0), -1.2, 1.2),
        "initial_state": jnp.clip(jax.random.uniform(seeds[1], (NROWS, NCOL), jnp.float32, -1.0, 1.0) * block_levels(seeds[1], (NROWS, NCOL), ((0, 8),), -0.4, 0.0), -1.0, 1.0),
        "residual": draw_residual(jax.random.fold_in(seeds[4], 71), 0),
        "mobility": jnp.clip(jnp.exp(math.log(200.0) - 2.3025851 * jax.random.uniform(seeds[3], (NROWS, NCOL), jnp.float32) ** block_levels(seeds[3], (NROWS, NCOL), ((0, 8),), -0.2, 0.2)), 20.0, 200.0),
    }


circ_weight = 0.2
time_step = 0.01
damping = 0.8
reaction_scale = 40.0

def time_tables(step_count):
    positions = jnp.arange(step_count).astype(jnp.float32)
    pair_ids = jnp.arange(step_count // 2).astype(jnp.float32)
    phases = 2.0 * jnp.pi * pair_ids / step_count
    angles = phases[:, None] * positions[None, :]
    forward = jnp.stack([jnp.cos(angles), -jnp.sin(angles)], axis=1).reshape(step_count, step_count)
    row_id = jnp.arange(step_count)[:, None]
    forward = jnp.where(row_id == 1, jnp.cos(jnp.pi * positions)[None, :], forward)
    scaling = jnp.where(jnp.arange(step_count) < 2, 1.0, 2.0) / step_count
    inverse = forward.T * scaling[None, :]
    factor = circ_weight ** (1.0 / step_count)
    shift_pair = (1.0 - factor * jnp.cos(phases)) / time_step
    shifts = jnp.stack([shift_pair, shift_pair], axis=1).reshape(step_count)
    shifts = shifts.at[1].set((1.0 + factor) / time_step)
    coupling = factor * jnp.sin(phases) / time_step
    signed = jnp.stack([-coupling, coupling], axis=1).reshape(step_count)
    weights = circ_weight ** (positions / step_count)
    return (forward, inverse, shifts, signed, weights)

def neg_laplace(values):
    neighbours = jnp.roll(values, 1, axis=1) + jnp.roll(values, -1, axis=1)
    neighbours = neighbours + jnp.roll(values, 1, axis=2) + jnp.roll(values, -1, axis=2)
    return 4.0 * values - neighbours

def partner(values):
    extent = values.shape
    return jnp.flip(values.reshape(extent[0] // 2, 2, extent[1], extent[2]), axis=1).reshape(extent)

def relax_pairs(spectrum, shifts, signed, frozen, mobility):
    shift_col = shifts[:, None, None]
    signed_col = signed[:, None, None]
    diagonal = shift_col + (frozen + 4.0 * mobility)[None]
    partner_diag = partner(diagonal)
    denominator = diagonal * partner_diag + signed_col * signed_col

    def one_sweep(sweep_id, values):
        applied = (shift_col + frozen[None]) * values + mobility[None] * neg_laplace(values) + signed_col * partner(values)
        defect = spectrum - applied
        return values + damping * (partner_diag * defect - signed_col * partner(defect)) / denominator
    return lax.fori_loop(0, SWEEPS, one_sweep, jnp.zeros_like(spectrum))

def precondition(values, frozen, mobility, tables):
    forward, inverse, shifts, signed, weights = tables
    weighted = weights[:, None, None] * values
    spectrum = jnp.einsum('mj,jrc->mrc', forward, weighted, precision=lax.Precision.HIGHEST)
    solved = relax_pairs(spectrum, shifts, signed, frozen, mobility)
    restored = jnp.einsum('jm,mrc->jrc', inverse, solved, precision=lax.Precision.HIGHEST)
    return restored / weights[:, None, None]

def jacobian(values, trajectory, mobility):
    earlier = jnp.concatenate([jnp.zeros_like(values[:1]), values[:-1]], axis=0)
    reaction = reaction_scale * (3.0 * trajectory * trajectory - 1.0)
    return (values - earlier) / time_step + mobility[None] * neg_laplace(values) + reaction * values

def reference(trajectory, initial_state, residual, mobility):
    tables = time_tables(NT)
    frozen = reaction_scale * jnp.maximum(3.0 * initial_state * initial_state - 1.0, 0.0)
    norm_value = jnp.sqrt(jnp.sum(residual * residual))
    unit_residual = residual / norm_value
    direction = precondition(unit_residual, frozen, mobility, tables)
    applied = jacobian(direction, trajectory, mobility)
    projection = jnp.sum(unit_residual * applied)
    rest_part = applied - projection * unit_residual
    remainder = jnp.sum(rest_part * rest_part)
    squared_sum = projection * projection + remainder
    update = norm_value * projection / squared_sum * direction
    reduction = jnp.sqrt(remainder / squared_sum)
    return (update, reduction)
```

```python
import functools

import jax
import jax.numpy as jnp
import ml_dtypes
import numpy as np
from jax import lax
from jax.experimental import pallas as pl
from jax.experimental.pallas import tpu as pltpu
from jax.sharding import Mesh
from jax.sharding import PartitionSpec as P

NT = 64
SPACE = ("space_0", "space_1")
TM = ("tm_0", "tm_1")
NTM = 16
NSP = 8
STEPS = NT // NTM
ROWS = 64
COLS = 1024
HALO = 16
WIDE = ROWS + 2 * HALO
PAD = WIDE + 8
FIRST = HALO - 1
KEPT = ROWS + 2
GROUPS = 4
BLOCK = 8
GROUP_SETS = ((0, 1), (2, 3))

circ_weight = 0.2
time_step = 0.01
reaction_scale = 40.0

F32 = jnp.float32
BF16 = jnp.bfloat16
VMEM_LIMIT = 56 * 1024 * 1024


def time_tables():
    steps = np.arange(NT)
    theta = 2.0 * np.pi * np.arange(NT // 2) / NT
    angles = theta[:, None] * steps[None, :]
    forward = np.stack([np.cos(angles), -np.sin(angles)], axis=1).reshape(NT, NT)
    forward[1] = np.cos(np.pi * steps)
    inverse = forward.T * (np.where(steps < 2, 1.0, 2.0) / NT)[None, :]
    factor = circ_weight ** (1.0 / NT)
    shifts = np.repeat((1.0 - factor * np.cos(theta)) / time_step, 2)
    shifts[1] = (1.0 + factor) / time_step
    coupling = np.repeat(-factor * np.sin(theta) / time_step, 2)
    weights = circ_weight ** (steps / NT)
    step_order = np.array([4 * src + q for q in range(4) for src in range(16)])
    coef_order = np.array(
        [2 * (8 * g + p) + half for g in range(GROUPS) for half in range(2) for p in range(8)]
    )
    forward = (forward * weights[None, :])[coef_order][:, step_order]
    inverse = (inverse / weights[:, None])[step_order][:, coef_order]
    wide = lambda v: np.repeat(v[coef_order][:, None], 128, axis=1).astype(np.float32)
    return split_matrix(forward), split_matrix(inverse), wide(shifts), wide(coupling)


def split_matrix(matrix):
    high = matrix.astype(ml_dtypes.bfloat16)
    low = (matrix - high.astype(np.float64)).astype(ml_dtypes.bfloat16)
    return np.concatenate([high, high, low, low], axis=1)


def transform(matrix, values):
    high = values.astype(BF16)
    low = (values - high.astype(F32)).astype(BF16)
    stacked = jnp.concatenate([high, low, high, low], axis=0)
    return jnp.dot(matrix, stacked, preferred_element_type=F32)


def lanes(rows=8):
    return lax.broadcasted_iota(jnp.int32, (rows, 128), 1)


def roll(values, shift):
    shift %= 128
    return values if shift == 0 else pltpu.roll(values, shift, 1)


def pack_kernel(with_halo, in_ref, out_ref):
    lane = lanes()
    low_half = lane < 64
    slot = lane // 16

    def rows_body(i, _):
        rows = pl.ds(pl.multiple_of(i * 8, 8), 8)
        v = [[in_ref[t, rows, 128 * k : 128 * k + 128] for k in range(8)] for t in range(4)]
        for b in range(NTM):
            k = b // 2
            for j in range(2):
                first, second = v[2 * j][k], v[2 * j + 1][k]
                if b % 2 == 0:
                    second = roll(second, 64)
                else:
                    first = roll(first, 64)
                out_ref[b, j, rows, :] = jnp.where(low_half, first, second)
            if with_halo:
                halo = None
                for t in range(4):
                    if b % 2 == 0:
                        both = jnp.where(lane < 112, v[t][k], v[t][(k - 1) % 8])
                        both = roll(both, (2 * t - 4) * 16)
                    else:
                        both = jnp.where(lane < 16, v[t][(k + 1) % 8], v[t][k])
                        both = roll(both, 2 * t * 16)
                    if halo is None:
                        halo = both
                    else:
                        mine = (slot == 2 * t) | (slot == (2 * t + 3) % 8)
                        halo = jnp.where(mine, both, halo)
                out_ref[b, 2, rows, :] = halo
        return 0

    lax.fori_loop(0, ROWS // 8, rows_body, 0)


def pack(array, with_halo):
    slabs = 3 if with_halo else 2
    return pl.pallas_call(
        functools.partial(pack_kernel, with_halo),
        out_shape=jax.ShapeDtypeStruct((NTM, slabs, ROWS, 128), F32),
        compiler_params=pltpu.CompilerParams(vmem_limit_bytes=VMEM_LIMIT),
        name="pack_halo" if with_halo else "pack",
    )(array)


def steps_tile(ref, row, rows, slabs, low_half):
    tiles = []
    loaded = [ref[pl.ds(row + rows * j, NTM, stride=rows * slabs), :] for j in range(slabs)]
    for q in range(4):
        own = roll(loaded[q // 2], 64 * (q % 2))
        if slabs == 3:
            own = jnp.where(low_half, own, roll(loaded[2], 64 - 32 * q))
        tiles.append(own)
    return jnp.concatenate(tiles, axis=0)


def solve_kernel(
    x_ref, low_ref, high_ref, mob_ref, ini_ref, fwd_ref, inv_ref, shift_ref, couple_ref,
    out_ref, dir_ref, s_ref, u_ref, w_ref, p_ref, q_ref, pb_ref,
):
    low_half = lanes(NTM) < 64

    def spectrum(source, rows, offset):
        def pair_body(i, _):
            first = 2 * i
            x = jnp.concatenate(
                [steps_tile(source, first + e, rows, 3, low_half) for e in range(2)], axis=1
            )
            coefs = transform(fwd_ref[...], x)
            for e in range(2):
                row = first + e + offset
                mob = jnp.broadcast_to(mob_ref[pl.ds(row, 1), :], (8, 128))
                ini = jnp.broadcast_to(ini_ref[pl.ds(row, 1), :], (8, 128))
                frozen = reaction_scale * jnp.maximum(3.0 * ini * ini - 1.0, 0.0)
                base = frozen + 4.0 * mob
                for g in range(GROUPS):
                    a, b = 16 * g, 16 * g + 8
                    s_a = coefs[a : a + 8, 128 * e : 128 * e + 128]
                    s_b = coefs[b : b + 8, 128 * e : 128 * e + 128]
                    c = couple_ref[a : a + 8, :]
                    diag_a = shift_ref[a : a + 8, :] + base
                    diag_b = shift_ref[b : b + 8, :] + base if g == 0 else diag_a
                    scale = 0.8 / (diag_a * diag_b + c * c)
                    k_a = diag_b * scale
                    k_b = diag_a * scale
                    k_c = c * scale
                    s_ref[row, a : a + 8, :] = k_a * s_a - k_c * s_b
                    s_ref[row, b : b + 8, :] = k_b * s_b + k_c * s_a
                    mob5 = 5.0 * mob
                    p_ref[row, 8 * g : 8 * g + 8, :] = mob5 * k_a
                    q_ref[row, 8 * g : 8 * g + 8, :] = mob5 * k_c
                    if g == 0:
                        pb_ref[row, :, :] = mob5 * k_b
            return 0

        lax.fori_loop(0, rows // 2, pair_body, 0)

    spectrum(low_ref, HALO, 0)
    spectrum(x_ref, ROWS, HALO)
    spectrum(high_ref, HALO, HALO + ROWS)

    def apply(k, source, target, join=None, old=None):
        count = WIDE - 2 * k

        for groups in GROUP_SETS:
            tiles = [16 * g + 8 * half for g in groups for half in range(2)]

            def load(row):
                return [source[row, m : m + 8, :] for m in tiles]

            def diagonal(here, below):
                return [h + roll(b, -1) for h, b in zip(here, below)]

            def body(i, carry):
                here, diag = carry
                start = k + i * BLOCK
                for e in range(BLOCK):
                    row = start + e
                    below = load(row + 1)
                    diag_now = diagonal(here, below)
                    n = [up + roll(d, 1) for up, d in zip(diag, diag_now)]
                    for j, g in enumerate(groups):
                        n_a, n_b = n[2 * j], n[2 * j + 1]
                        p = p_ref[row, 8 * g : 8 * g + 8, :]
                        q = q_ref[row, 8 * g : 8 * g + 8, :]
                        p_b = pb_ref[row, :, :] if g == 0 else p
                        new = [
                            here[2 * j] + (p * n_a - q * n_b),
                            here[2 * j + 1] + (p_b * n_b + q * n_a),
                        ]
                        for half in range(2):
                            m = tiles[2 * j + half]
                            value = new[half]
                            if join is not None:
                                kept = here[2 * j + half] if old is source else old[row, m : m + 8, :]
                                value = kept + join * value
                            target[row, m : m + 8, :] = value
                    here, diag = below, diag_now
                return here, diag

            above, here = load(k - 1), load(k)
            lax.fori_loop(0, -(-count // BLOCK), body, (list(here), diagonal(above, here)))

    apply(1, s_ref, u_ref, 0.2, s_ref)
    k = 1
    for power in (2, 4, 8):
        source = u_ref
        for step in range(power - 1):
            k += 1
            target = (s_ref, w_ref)[step % 2]
            apply(k, source, target)
            source = target
        k += 1
        apply(k, source, u_ref, 0.2**power, u_ref)

    def back_body(i, _):
        y = jnp.concatenate([u_ref[FIRST + 2 * i + e] for e in range(2)], axis=1)
        values = transform(inv_ref[...], y)
        for e in range(2):
            dir_ref[2 * i + e] = values[:, 128 * e : 128 * e + 128]
        return 0

    lax.fori_loop(0, KEPT // 2, back_body, 0)

    def out_body(r, _):
        v = dir_ref[r + 1]
        for j in range(2):
            first = v[32 * j : 32 * j + 16]
            second = roll(v[32 * j + 16 : 32 * j + 32], 64)
            out_ref[pl.ds(r + ROWS * j, NTM, stride=2 * ROWS), :] = jnp.where(low_half, first, second)
        return 0

    lax.fori_loop(0, ROWS, out_body, 0)


def solve(x, low, high, mob, ini):
    forward, inverse, shifts, coupling = time_tables()
    wide = pltpu.VMEM((PAD, NT, 128), F32)
    half = pltpu.VMEM((PAD, NT // 2, 128), F32)
    return pl.pallas_call(
        solve_kernel,
        out_shape=(
            jax.ShapeDtypeStruct((NTM * 2 * ROWS, 128), F32),
            jax.ShapeDtypeStruct((KEPT, NT, 128), F32),
        ),
        scratch_shapes=[wide, wide, wide, half, half, pltpu.VMEM((PAD, 8, 128), F32)],
        compiler_params=pltpu.CompilerParams(vmem_limit_bytes=VMEM_LIMIT),
        name="solve",
    )(x, low, high, mob, ini, forward, inverse, shifts, coupling)


def jacobian_kernel(dir_ref, traj_ref, x_ref, mob_ref, out_ref):
    first_row = lax.broadcasted_iota(jnp.int32, (NTM, 128), 0) == 0

    def own(ref, row, slabs):
        loaded = [ref[pl.ds(row + ROWS * j, NTM, stride=ROWS * slabs), :] for j in range(2)]
        return jnp.concatenate([roll(loaded[q // 2], 64 * (q % 2)) for q in range(4)], axis=0)

    def fold(values):
        return functools.reduce(jnp.add, [values[8 * i : 8 * i + 8] for i in range(8)])

    def body(r, sums):
        v = dir_ref[r + 1]
        neighbours = (dir_ref[r] + dir_ref[r + 2]) + (roll(v, 1) + roll(v, -1))
        carried = jnp.where(first_row, 0.0, pltpu.roll(v[48:64], 1, 0))
        earlier = jnp.concatenate([carried, v[:48]], axis=0)
        mob = mob_ref[pl.ds(r + HALO, 1), :]
        traj = own(traj_ref, r, 2)
        res = own(x_ref, r, 3)
        reaction = reaction_scale * (3.0 * traj * traj - 1.0)
        applied = (v - earlier) / time_step + mob * (4.0 * v - neighbours) + reaction * v
        new = (res * res, res * applied, applied * applied)
        return tuple(s + fold(n) for s, n in zip(sums, new))

    zero = jnp.zeros((8, 128), F32)
    sums = lax.fori_loop(0, ROWS, body, (zero, zero, zero))
    totals = [jnp.sum(jnp.where(lanes() < 64, s, 0.0)) for s in sums]
    row = lax.broadcasted_iota(jnp.int32, (8, 128), 0)
    out_ref[...] = jnp.where(row == 0, totals[0], jnp.where(row == 1, totals[1], totals[2]))


def jacobian_sums(direction, traj, x, mob):
    return pl.pallas_call(
        jacobian_kernel,
        out_shape=jax.ShapeDtypeStruct((8, 128), F32),
        compiler_params=pltpu.CompilerParams(vmem_limit_bytes=VMEM_LIMIT),
        name="jacobian_sums",
    )(direction, traj, x, mob)


def finish_kernel(blocks_ref, sums_ref, out_ref):
    low_half = lanes() < 64
    row = lambda i: jnp.broadcast_to(sums_ref[i : i + 1, :], (8, 128))
    scale = row(1) / row(2)

    def body(i, _):
        rows = pl.ds(pl.multiple_of(i * 8, 8), 8)
        for k in range(8):
            for j in range(2):
                even = blocks_ref[2 * k, j, rows, :] * scale
                odd = blocks_ref[2 * k + 1, j, rows, :] * scale
                lane = slice(128 * k, 128 * k + 128)
                out_ref[2 * j, rows, lane] = jnp.where(low_half, even, roll(odd, 64))
                out_ref[2 * j + 1, rows, lane] = jnp.where(low_half, roll(even, 64), odd)
        return 0

    lax.fori_loop(0, ROWS // 8, body, 0)


def finish(blocks, sums):
    return pl.pallas_call(
        finish_kernel,
        out_shape=jax.ShapeDtypeStruct((STEPS, ROWS, COLS), F32),
        compiler_params=pltpu.CompilerParams(vmem_limit_bytes=VMEM_LIMIT),
        name="finish",
    )(blocks, sums)


def swap(blocks):
    return lax.all_to_all(blocks, TM, split_axis=0, concat_axis=0, tiled=True)


def shifted(array, axes, size, distance):
    return lax.ppermute(array, axes, [(i, (i + distance) % size) for i in range(size)])


def row_halos(array, dim):
    last = lax.slice_in_dim(array, ROWS - HALO, ROWS, axis=dim)
    first = lax.slice_in_dim(array, 0, HALO, axis=dim)
    return shifted(last, SPACE, NSP, 1), shifted(first, SPACE, NSP, -1)


def own_columns(array):
    block = lax.axis_index(TM)
    padded = jnp.concatenate([array[:, :, -128:], array, array[:, :, :128]], axis=2)
    here = lax.dynamic_slice_in_dim(padded, 64 * block + 128, 128, axis=2)
    before = lax.dynamic_slice_in_dim(padded, 64 * block, 128, axis=2)
    return jnp.where(jnp.arange(128) < 112, here, before)


def total(sums):
    sums = sums + shifted(sums, "space_1", 2, 1)
    for axis in ("space_0", "tm_1", "tm_0"):
        one, two, three = (shifted(sums, axis, 4, d) for d in (1, 2, 3))
        sums = (sums + two) + (one + three)
    return sums


def on_device(trajectory, initial_state, residual, mobility):
    x = swap(pack(residual, True))
    low, high = row_halos(x, 2)
    fields = own_columns(jnp.stack([mobility, initial_state]))
    below, above = row_halos(fields, 1)
    mob, ini = jnp.concatenate([below, fields, above], axis=1)
    traj = swap(pack(trajectory, False))
    flat = lambda a: a.reshape(-1, 128)
    packed, direction = solve(flat(x), flat(low), flat(high), mob, ini)
    blocks = swap(packed.reshape(NTM, 2, ROWS, 128))
    sums = total(jacobian_sums(direction, flat(traj), flat(x), mob))
    norm_square, cross_sum, squared_applied = sums[0, 0], sums[1, 0], sums[2, 0]
    projection = cross_sum / norm_square
    squared_sum = squared_applied / norm_square
    remainder = jnp.maximum(squared_sum - projection * projection, 0.0)
    return finish(blocks, sums), jnp.sqrt(remainder / squared_sum)


def solution(mesh):
    torus = Mesh(mesh.devices.reshape(4, 4, 4, 2), TM + SPACE)
    in_specs = (P(TM, SPACE, None), P(SPACE, None), P(TM, SPACE, None), P(SPACE, None))
    out_specs = (P(TM, SPACE, None), P())
    return jax.shard_map(
        on_device, mesh=torus, in_specs=in_specs, out_specs=out_specs, check_vma=False
    )
```

```python
import functools

import jax
import jax.numpy as jnp
import ml_dtypes
import numpy as np
from jax import lax
from jax.experimental import pallas as pl
from jax.experimental.pallas import tpu as pltpu
from jax.sharding import Mesh
from jax.sharding import PartitionSpec as P

NT = 64
SPACE = ("space_0", "space_1")
TM = ("tm_0", "tm_1")
NTM = 16
NSP = 8
STEPS = NT // NTM
ROWS = 64
COLS = 1024
HALO = 16
WIDE = ROWS + 2 * HALO
PAD = WIDE + 16
FIRST = HALO - 1
KEPT = ROWS + 2
GROUPS = 4
BLOCK = 16
BATCH = 8
JBATCH = 4

circ_weight = 0.2
time_step = 0.01
reaction_scale = 40.0

F32 = jnp.float32
BF16 = jnp.bfloat16
VMEM_LIMIT = 56 * 1024 * 1024


def time_tables():
    steps = np.arange(NT)
    theta = 2.0 * np.pi * np.arange(NT // 2) / NT
    angles = theta[:, None] * steps[None, :]
    forward = np.stack([np.cos(angles), -np.sin(angles)], axis=1).reshape(NT, NT)
    forward[1] = np.cos(np.pi * steps)
    inverse = forward.T * (np.where(steps < 2, 1.0, 2.0) / NT)[None, :]
    factor = circ_weight ** (1.0 / NT)
    shifts = np.repeat((1.0 - factor * np.cos(theta)) / time_step, 2)
    shifts[1] = (1.0 + factor) / time_step
    coupling = np.repeat(-factor * np.sin(theta) / time_step, 2)
    weights = circ_weight ** (steps / NT)
    step_order = np.array([4 * src + q for q in range(4) for src in range(16)])
    coef_order = np.array(
        [2 * (8 * g + p) + half for g in range(GROUPS) for half in range(2) for p in range(8)]
    )
    forward = (forward * weights[None, :])[coef_order][:, step_order]
    inverse = (inverse / weights[:, None])[step_order][:, coef_order]
    by_pair = lambda v: np.repeat(v.reshape(GROUPS, 8).T, 32, axis=1)
    coefs = [by_pair(shifts[0::2]), by_pair(shifts[1::2]), by_pair(coupling[0::2])]
    return split_matrix(forward), split_matrix(inverse), np.stack(coefs).astype(np.float32)


def split_matrix(matrix):
    high = matrix.astype(ml_dtypes.bfloat16)
    low = (matrix - high.astype(np.float64)).astype(ml_dtypes.bfloat16)
    return np.concatenate([high, high, low, low], axis=1)


def transform(matrix, values):
    high = values.astype(BF16)
    low = (values - high.astype(F32)).astype(BF16)
    stacked = jnp.concatenate([high, low, high, low], axis=0)
    return jnp.dot(matrix, stacked, preferred_element_type=F32)


def lanes(rows=8):
    return lax.broadcasted_iota(jnp.int32, (rows, 128), 1)


def roll(values, shift):
    shift %= 128
    return values if shift == 0 else pltpu.roll(values, shift, 1)


def permute_lanes(values, index):
    return jnp.take_along_axis(values, index, axis=1, mode="promise_in_bounds")


def pack_kernel(in_ref, out_ref):
    low_half = lanes() < 64

    def rows_body(i, _):
        rows = pl.ds(pl.multiple_of(i * 8, 8), 8)
        for k in range(8):
            for j in range(2):
                lane = slice(128 * k, 128 * k + 128)
                first, second = in_ref[2 * j, rows, lane], in_ref[2 * j + 1, rows, lane]
                out_ref[2 * k, j, rows, :] = jnp.where(low_half, first, roll(second, 64))
                out_ref[2 * k + 1, j, rows, :] = jnp.where(low_half, roll(first, 64), second)
        return 0

    lax.fori_loop(0, ROWS // 8, rows_body, 0)


def pack_halo_kernel(in_ref, out_ref):
    lane = lanes()
    slot, q = lane // 32, lane % 32

    def rows_body(i, _):
        rows = pl.ds(pl.multiple_of(i * 8, 8), 8)
        for odd in range(2):
            base = 48 if odd else -16
            index = [(3 * q + jnp.where(slot < 3, slot, j) + base) & 127 for j in range(3)]
            for b in range(odd, NTM, 2):
                k = b // 2
                both = []
                for t in range(4):
                    v = lambda k: in_ref[t, rows, 128 * (k % 8) : 128 * (k % 8) + 128]
                    if odd:
                        both.append(jnp.where(lane < 16, v(k + 1), v(k)))
                    else:
                        both.append(jnp.where(lane < 112, v(k), v(k - 1)))
                for j in range(3):
                    source = permute_lanes(both[j], index[j])
                    out_ref[b, j, rows, :] = jnp.where(
                        slot < 3, source, permute_lanes(both[3], index[j])
                    )
        return 0

    lax.fori_loop(0, ROWS // 8, rows_body, 0)


def pack(array, kernel, slabs, name):
    return pl.pallas_call(
        kernel,
        out_shape=jax.ShapeDtypeStruct((NTM, slabs, ROWS, 128), F32),
        compiler_params=pltpu.CompilerParams(vmem_limit_bytes=VMEM_LIMIT),
        name=name,
    )(array)


def halo_tiles(ref, row, rows, slot):
    slabs = [ref[pl.ds(row + rows * j, NTM, stride=3 * rows), :] for j in range(3)]
    last = jnp.where(slot == 0, roll(slabs[0], 32), jnp.where(slot == 1, roll(slabs[1], 64), roll(slabs[2], 96)))
    return slabs + [last]


def swap_blocks(d, slot, count):
    low_half, even = slot < 2, slot % 2 == 0
    d0 = jnp.where(low_half, d[0], roll(d[2], 64))
    d1 = jnp.where(low_half, d[1], roll(d[3], 64))
    d2 = jnp.where(low_half, roll(d[0], 64), d[2])
    d3 = jnp.where(low_half, roll(d[1], 64), d[3])
    out = [
        jnp.where(even, d0, roll(d1, 32)),
        jnp.where(even, roll(d0, -32), d1),
        jnp.where(even, d2, roll(d3, 32)),
    ]
    if count == 4:
        out.append(jnp.where(even, roll(d2, -32), d3))
    return out


def natural_index(rows):
    lane = lanes(rows)
    column = jnp.where(lane < 80, lane + 16, jnp.where(lane < 112, 0, lane - 112))
    return 32 * (column % 3) + column // 3


def solve_kernel(
    x_ref, low_ref, high_ref, mob_ref, ini_ref, fwd_ref, inv_ref, coef_ref,
    out_ref, dir_ref, s_ref, u_ref, w_ref, pa_ref, pb_ref, q_ref,
):
    slot = lanes() // 32
    slot16 = lanes(NTM) // 32

    def spectrum(source, rows, offset):
        def body(i, _):
            first = i * BATCH
            x = [
                jnp.concatenate(halo_tiles(source, first + e, rows, slot16), axis=0)
                for e in range(BATCH)
            ]
            coefs = transform(fwd_ref[...], jnp.concatenate(x, axis=1))
            c = coef_ref[2]
            for e in range(BATCH):
                row = first + e + offset
                here = coefs[:, 128 * e : 128 * e + 128]
                parts = [
                    swap_blocks([here[16 * g + 8 * h : 16 * g + 8 * h + 8] for g in range(4)], slot, 3)
                    for h in range(2)
                ]
                for k in range(3):
                    mob = jnp.broadcast_to(mob_ref[k, pl.ds(row, 1), :], (8, 128))
                    ini = jnp.broadcast_to(ini_ref[k, pl.ds(row, 1), :], (8, 128))
                    frozen = reaction_scale * jnp.maximum(3.0 * ini * ini - 1.0, 0.0)
                    base = frozen + 4.0 * mob
                    diag_a = coef_ref[0] + base
                    diag_b = coef_ref[1] + base
                    scale = 0.8 / (diag_a * diag_b + c * c)
                    k_a, k_b, k_c = diag_b * scale, diag_a * scale, c * scale
                    s_a, s_b = parts[0][k], parts[1][k]
                    s_ref[row, 16 * k : 16 * k + 8, :] = k_a * s_a - k_c * s_b
                    s_ref[row, 16 * k + 8 : 16 * k + 16, :] = k_b * s_b + k_c * s_a
                    mob5 = 5.0 * mob
                    tile = slice(8 * k, 8 * k + 8)
                    pa_ref[row, tile, :] = mob5 * k_a
                    pb_ref[row, tile, :] = mob5 * k_b
                    q_ref[row, tile, :] = mob5 * k_c
            return 0

        lax.fori_loop(0, rows // BATCH, body, 0)

    spectrum(low_ref, HALO, 0)
    spectrum(x_ref, ROWS, HALO)
    spectrum(high_ref, HALO, HALO + ROWS)

    def apply(k, source, target, join=None, old=None):
        count = WIDE - 2 * k

        def load(row):
            return [source[row, 8 * m : 8 * m + 8, :] for m in range(6)]

        def body(i, carry):
            above, here = carry
            start = k + i * BLOCK
            for e in range(BLOCK):
                row = start + e
                below = load(row + 1)
                n = [a + b for a, b in zip(above, below)]
                for h in range(2):
                    t0, t1, t2 = here[h], here[2 + h], here[4 + h]
                    n[h] += roll(t2, 1) + t1
                    n[2 + h] += t0 + t2
                    n[4 + h] += t1 + roll(t0, -1)
                for j in range(3):
                    tile = slice(8 * j, 8 * j + 8)
                    p_a, p_b, q = pa_ref[row, tile, :], pb_ref[row, tile, :], q_ref[row, tile, :]
                    n_a, n_b = n[2 * j], n[2 * j + 1]
                    new = [
                        here[2 * j] + (p_a * n_a - q * n_b),
                        here[2 * j + 1] + (p_b * n_b + q * n_a),
                    ]
                    for h in range(2):
                        m = slice(16 * j + 8 * h, 16 * j + 8 * h + 8)
                        value = new[h]
                        if join is not None:
                            kept = here[2 * j + h] if old is source else old[row, m, :]
                            value = kept + join * value
                        target[row, m, :] = value
                above, here = here, below
            return above, here

        lax.fori_loop(0, -(-count // BLOCK), body, (load(k - 1), load(k)))

    apply(1, s_ref, u_ref, 0.2, s_ref)
    k = 1
    for power in (2, 4, 8):
        source = u_ref
        for step in range(power - 1):
            k += 1
            target = (s_ref, w_ref)[step % 2]
            apply(k, source, target)
            source = target
        k += 1
        apply(k, source, u_ref, 0.2**power, u_ref)

    natural = natural_index(NT)
    low_half = lanes(NTM) < 64

    def back(rows):
        y = []
        for row in rows:
            halves = []
            for h in range(2):
                t = [u_ref[row + FIRST, 16 * k + 8 * h : 16 * k + 8 * h + 8, :] for k in range(3)]
                halves.append(swap_blocks(t + [t[2]], slot, 4))
            y.append(jnp.concatenate([halves[h][g] for g in range(4) for h in range(2)], axis=0))
        values = transform(inv_ref[...], jnp.concatenate(y, axis=1))
        out = []
        for e, row in enumerate(rows):
            v = permute_lanes(values[:, 128 * e : 128 * e + 128], natural)
            dir_ref[row] = v
            out.append(v)
        return out

    back([0, KEPT - 1])

    def back_body(i, _):
        for e, v in enumerate(back([i * BATCH + e + 1 for e in range(BATCH)])):
            for j in range(2):
                both = jnp.where(low_half, v[32 * j : 32 * j + 16], roll(v[32 * j + 16 : 32 * j + 32], 64))
                out_ref[pl.ds(i * BATCH + e + ROWS * j, NTM, stride=2 * ROWS), :] = both
        return 0

    lax.fori_loop(0, ROWS // BATCH, back_body, 0)


def solve(x, low, high, mob, ini):
    wide = pltpu.VMEM((PAD, 48, 128), F32)
    half = pltpu.VMEM((PAD, 24, 128), F32)
    return pl.pallas_call(
        solve_kernel,
        out_shape=(
            jax.ShapeDtypeStruct((NTM * 2 * ROWS, 128), F32),
            jax.ShapeDtypeStruct((KEPT, NT, 128), F32),
        ),
        scratch_shapes=[wide, wide, wide, half, half, half],
        compiler_params=pltpu.CompilerParams(vmem_limit_bytes=VMEM_LIMIT),
        name="solve",
    )(x, low, high, mob, ini, *time_tables())


def jacobian_kernel(dir_ref, traj_ref, x_ref, mob_ref, out_ref):
    first_row = lax.broadcasted_iota(jnp.int32, (NTM, 128), 0) == 0

    natural = natural_index(NT)
    slot = lanes(NTM) // 32

    def own(ref, row):
        slabs = [ref[pl.ds(row + ROWS * j, NTM, stride=2 * ROWS), :] for j in range(2)]
        return jnp.concatenate([roll(slabs[q // 2], 64 * (q % 2)) for q in range(4)], axis=0)

    def fold(values):
        return functools.reduce(jnp.add, [values[8 * i : 8 * i + 8] for i in range(8)])

    def one_row(r):
        v = dir_ref[r + 1]
        neighbours = (dir_ref[r] + dir_ref[r + 2]) + (roll(v, 1) + roll(v, -1))
        carried = jnp.where(first_row, 0.0, pltpu.roll(v[48:64], 1, 0))
        earlier = jnp.concatenate([carried, v[:48]], axis=0)
        mob = mob_ref[pl.ds(r + HALO, 1), :]
        traj = own(traj_ref, r)
        res = jnp.concatenate(halo_tiles(x_ref, r, ROWS, slot), axis=0)
        res = permute_lanes(res, natural)
        reaction = reaction_scale * (3.0 * traj * traj - 1.0)
        applied = (v - earlier) / time_step + mob * (4.0 * v - neighbours) + reaction * v
        return [fold(p) for p in (res * res, res * applied, applied * applied)]

    def body(i, sums):
        parts = [one_row(i * JBATCH + e) for e in range(JBATCH)]
        return tuple(s + functools.reduce(jnp.add, p) for s, p in zip(sums, zip(*parts)))

    zero = jnp.zeros((8, 128), F32)
    sums = lax.fori_loop(0, ROWS // JBATCH, body, (zero, zero, zero))
    totals = [jnp.sum(jnp.where(lanes() < 64, s, 0.0)) for s in sums]
    row = lax.broadcasted_iota(jnp.int32, (8, 128), 0)
    out_ref[...] = jnp.where(row == 0, totals[0], jnp.where(row == 1, totals[1], totals[2]))


def jacobian_sums(direction, traj, x, mob):
    return pl.pallas_call(
        jacobian_kernel,
        out_shape=jax.ShapeDtypeStruct((8, 128), F32),
        compiler_params=pltpu.CompilerParams(vmem_limit_bytes=VMEM_LIMIT),
        name="jacobian_sums",
    )(direction, traj, x, mob)


def finish_kernel(blocks_ref, sums_ref, out_ref):
    low_half = lanes() < 64
    row = lambda i: jnp.broadcast_to(sums_ref[i : i + 1, :], (8, 128))
    scale = row(1) / row(2)

    def body(i, _):
        rows = pl.ds(pl.multiple_of(i * 8, 8), 8)
        for k in range(8):
            for j in range(2):
                even = blocks_ref[2 * k, j, rows, :] * scale
                odd = blocks_ref[2 * k + 1, j, rows, :] * scale
                lane = slice(128 * k, 128 * k + 128)
                out_ref[2 * j, rows, lane] = jnp.where(low_half, even, roll(odd, 64))
                out_ref[2 * j + 1, rows, lane] = jnp.where(low_half, roll(even, 64), odd)
        return 0

    lax.fori_loop(0, ROWS // 8, body, 0)


def finish(blocks, sums):
    return pl.pallas_call(
        finish_kernel,
        out_shape=jax.ShapeDtypeStruct((STEPS, ROWS, COLS), F32),
        compiler_params=pltpu.CompilerParams(vmem_limit_bytes=VMEM_LIMIT),
        name="finish",
    )(blocks, sums)


def swap(blocks):
    return lax.all_to_all(blocks, TM, split_axis=0, concat_axis=0, tiled=True)


def shifted(array, axes, size, distance):
    return lax.ppermute(array, axes, [(i, (i + distance) % size) for i in range(size)])


def row_halos(array, dim):
    last = lax.slice_in_dim(array, ROWS - HALO, ROWS, axis=dim)
    first = lax.slice_in_dim(array, 0, HALO, axis=dim)
    return shifted(last, SPACE, NSP, 1), shifted(first, SPACE, NSP, -1)


def own_columns(array):
    block = lax.axis_index(TM)
    padded = jnp.concatenate([array[:, :, -HALO:], array, array[:, :, : HALO + 32]], axis=2)
    return lax.dynamic_slice_in_dim(padded, 64 * block, 128, axis=2)


def by_thirds(field):
    thirds = field[:, :96].reshape(WIDE, 32, 3).transpose(2, 0, 1)
    return jnp.concatenate([thirds] * GROUPS, axis=2)


def total(sums):
    sums = sums + shifted(sums, "space_1", 2, 1)
    for axis in ("space_0", "tm_1", "tm_0"):
        one, two, three = (shifted(sums, axis, 4, d) for d in (1, 2, 3))
        sums = (sums + two) + (one + three)
    return sums


def on_device(trajectory, initial_state, residual, mobility):
    x = swap(pack(residual, pack_halo_kernel, 3, "pack_halo"))
    low, high = row_halos(x, 2)
    fields = own_columns(jnp.stack([mobility, initial_state]))
    below, above = row_halos(fields, 1)
    mob, ini = jnp.concatenate([below, fields, above], axis=1)
    traj = swap(pack(trajectory, pack_kernel, 2, "pack"))
    flat = lambda a: a.reshape(-1, 128)
    packed, direction = solve(flat(x), flat(low), flat(high), by_thirds(mob), by_thirds(ini))
    blocks = swap(packed.reshape(NTM, 2, ROWS, 128))
    sums = total(jacobian_sums(direction, flat(traj), flat(x), jnp.roll(mob, -HALO, axis=1)))
    norm_square, cross_sum, squared_applied = sums[0, 0], sums[1, 0], sums[2, 0]
    projection = cross_sum / norm_square
    squared_sum = squared_applied / norm_square
    remainder = jnp.maximum(squared_sum - projection * projection, 0.0)
    return finish(blocks, sums), jnp.sqrt(remainder / squared_sum)


def solution(mesh):
    torus = Mesh(mesh.devices.reshape(4, 4, 4, 2), TM + SPACE)
    in_specs = (P(TM, SPACE, None), P(SPACE, None), P(TM, SPACE, None), P(SPACE, None))
    out_specs = (P(TM, SPACE, None), P())
    return jax.shard_map(
        on_device, mesh=torus, in_specs=in_specs, out_specs=out_specs, check_vma=False
    )
```

```python
import functools

import jax
import jax.numpy as jnp
import ml_dtypes
import numpy as np
from jax import lax
from jax.experimental import pallas as pl
from jax.experimental.pallas import tpu as pltpu
from jax.sharding import Mesh
from jax.sharding import PartitionSpec as P

NT = 64
SPACE = ("space_0", "space_1")
TM = ("tm_0", "tm_1")
NTM = 16
NSP = 8
STEPS = NT // NTM
ROWS = 64
COLS = 1024
HALO = 16
WIDE = ROWS + 2 * HALO
PAD = WIDE + 16
FIRST = HALO - 1
KEPT = ROWS + 2
GROUPS = 4
BLOCK = 16
LAST_BLOCK = 11
BATCH = 8
PACK_ROWS = 16
JBATCH = 4

circ_weight = 0.2
time_step = 0.01
reaction_scale = 40.0

F32 = jnp.float32
BF16 = jnp.bfloat16
MIB = 1024 * 1024


def time_tables():
    steps = np.arange(NT)
    theta = 2.0 * np.pi * np.arange(NT // 2) / NT
    angles = theta[:, None] * steps[None, :]
    forward = np.stack([np.cos(angles), -np.sin(angles)], axis=1).reshape(NT, NT)
    forward[1] = np.cos(np.pi * steps)
    inverse = forward.T * (np.where(steps < 2, 1.0, 2.0) / NT)[None, :]
    factor = circ_weight ** (1.0 / NT)
    shifts = np.repeat((1.0 - factor * np.cos(theta)) / time_step, 2)
    shifts[1] = (1.0 + factor) / time_step
    coupling = np.repeat(-factor * np.sin(theta) / time_step, 2)
    weights = circ_weight ** (steps / NT)
    step_order = np.array([4 * src + q for q in range(4) for src in range(16)])
    coef_order = np.array(
        [2 * (8 * g + p) + half for g in range(GROUPS) for half in range(2) for p in range(8)]
    )
    forward = (forward * weights[None, :])[coef_order][:, step_order]
    inverse = (inverse / weights[:, None])[step_order][:, coef_order]
    by_pair = lambda v: np.repeat(v.reshape(GROUPS, 8).T, 32, axis=1)
    coefs = [by_pair(shifts[0::2]), by_pair(shifts[1::2]), by_pair(coupling[0::2])]
    return split_matrix(forward), split_matrix(inverse), np.stack(coefs).astype(np.float32)


def split_matrix(matrix):
    high = matrix.astype(ml_dtypes.bfloat16)
    low = (matrix - high.astype(np.float64)).astype(ml_dtypes.bfloat16)
    return np.concatenate([high, high, low, low], axis=1)


def transform(matrix, values):
    high = values.astype(BF16)
    low = (values - high.astype(F32)).astype(BF16)
    stacked = jnp.concatenate([high, low, high, low], axis=0)
    return jnp.dot(matrix, stacked, preferred_element_type=F32)


def lanes(rows=8):
    return lax.broadcasted_iota(jnp.int32, (rows, 128), 1)


def roll(values, shift):
    shift %= 128
    return values if shift == 0 else pltpu.roll(values, shift, 1)


def permute_lanes(values, index):
    return jnp.take_along_axis(values, index, axis=1, mode="promise_in_bounds")


def pack_kernel(in_ref, out_ref):
    low_half = lanes() < 64
    for rows in (slice(i, i + 8) for i in range(0, PACK_ROWS, 8)):
        for k in range(8):
            for j in range(2):
                lane = slice(128 * k, 128 * k + 128)
                first, second = in_ref[2 * j, rows, lane], in_ref[2 * j + 1, rows, lane]
                out_ref[2 * k, j, rows, :] = jnp.where(low_half, first, roll(second, 64))
                out_ref[2 * k + 1, j, rows, :] = jnp.where(low_half, roll(first, 64), second)


def pack_halo_kernel(in_ref, out_ref):
    lane = lanes()
    slot, q = lane // 32, lane % 32
    for rows in (slice(i, i + 8) for i in range(0, PACK_ROWS, 8)):
        for odd in range(2):
            base = 48 if odd else -16
            index = [(3 * q + jnp.where(slot < 3, slot, j) + base) & 127 for j in range(3)]
            for b in range(odd, NTM, 2):
                k = b // 2
                both = []
                for t in range(4):
                    v = lambda k: in_ref[t, rows, 128 * (k % 8) : 128 * (k % 8) + 128]
                    if odd:
                        both.append(jnp.where(lane < 16, v(k + 1), v(k)))
                    else:
                        both.append(jnp.where(lane < 112, v(k), v(k - 1)))
                for j in range(3):
                    source = permute_lanes(both[j], index[j])
                    out_ref[b, j, rows, :] = jnp.where(
                        slot < 3, source, permute_lanes(both[3], index[j])
                    )


def pack(array, kernel, slabs, name):
    return pl.pallas_call(
        kernel,
        grid=(ROWS // PACK_ROWS,),
        in_specs=[pl.BlockSpec((STEPS, PACK_ROWS, COLS), lambda i: (0, i, 0))],
        out_specs=pl.BlockSpec((NTM, slabs, PACK_ROWS, 128), lambda i: (0, 0, i, 0)),
        out_shape=jax.ShapeDtypeStruct((NTM, slabs, ROWS, 128), F32),
        compiler_params=pltpu.CompilerParams(vmem_limit_bytes=8 * MIB),
        name=name,
    )(array)


def vmem(*arrays):
    return [pltpu.with_memory_space_constraint(a, pltpu.VMEM) for a in arrays]


def halo_tiles(ref, row, rows, slot):
    slabs = [ref[pl.ds(row + rows * j, NTM, stride=3 * rows), :] for j in range(3)]
    last = jnp.where(slot == 0, roll(slabs[0], 32), jnp.where(slot == 1, roll(slabs[1], 64), roll(slabs[2], 96)))
    return slabs + [last]


def swap_blocks(d, slot, count):
    low_half, even = slot < 2, slot % 2 == 0
    d0 = jnp.where(low_half, d[0], roll(d[2], 64))
    d1 = jnp.where(low_half, d[1], roll(d[3], 64))
    d2 = jnp.where(low_half, roll(d[0], 64), d[2])
    d3 = jnp.where(low_half, roll(d[1], 64), d[3])
    out = [
        jnp.where(even, d0, roll(d1, 32)),
        jnp.where(even, roll(d0, -32), d1),
        jnp.where(even, d2, roll(d3, 32)),
    ]
    if count == 4:
        out.append(jnp.where(even, roll(d2, -32), d3))
    return out


def natural_index(rows):
    lane = lanes(rows)
    column = jnp.where(lane < 80, lane + 16, jnp.where(lane < 112, 0, lane - 112))
    return 32 * (column % 3) + column // 3


def spectrum(source, rows, offset, mob_ref, ini_ref, fwd_ref, coef_ref, s_ref, pa_ref, pb_ref, q_ref):
    slot = lanes() // 32
    slot16 = lanes(NTM) // 32

    def body(i, _):
        first = i * BATCH
        x = [
            jnp.concatenate(halo_tiles(source, first + e, rows, slot16), axis=0)
            for e in range(BATCH)
        ]
        coefs = transform(fwd_ref[...], jnp.concatenate(x, axis=1))
        c = coef_ref[2]
        for e in range(BATCH):
            row = first + e + offset
            here = coefs[:, 128 * e : 128 * e + 128]
            parts = [
                swap_blocks([here[16 * g + 8 * h : 16 * g + 8 * h + 8] for g in range(4)], slot, 3)
                for h in range(2)
            ]
            for k in range(3):
                mob = jnp.broadcast_to(mob_ref[k, pl.ds(row, 1), :], (8, 128))
                ini = jnp.broadcast_to(ini_ref[k, pl.ds(row, 1), :], (8, 128))
                frozen = reaction_scale * jnp.maximum(3.0 * ini * ini - 1.0, 0.0)
                base = frozen + 4.0 * mob
                diag_a = coef_ref[0] + base
                diag_b = coef_ref[1] + base
                scale = 0.8 / (diag_a * diag_b + c * c)
                k_a, k_b, k_c = diag_b * scale, diag_a * scale, c * scale
                s_a, s_b = parts[0][k], parts[1][k]
                s_ref[row, 16 * k : 16 * k + 8, :] = k_a * s_a - k_c * s_b
                s_ref[row, 16 * k + 8 : 16 * k + 16, :] = k_b * s_b + k_c * s_a
                mob5 = 5.0 * mob
                tile = slice(8 * k, 8 * k + 8)
                pa_ref[row, tile, :] = mob5 * k_a
                pb_ref[row, tile, :] = mob5 * k_b
                q_ref[row, tile, :] = mob5 * k_c
        return 0

    lax.fori_loop(0, rows // BATCH, body, 0)


def transform_kernel(x_ref, mob_ref, ini_ref, fwd_ref, coef_ref, *outs):
    spectrum(x_ref, ROWS, HALO, mob_ref, ini_ref, fwd_ref, coef_ref, *outs)


def sweep_kernel(
    low_ref, high_ref, mob_ref, ini_ref, fwd_ref, coef_ref, s_in, pa_in, pb_in, q_in,
    solved_ref, s_ref, pa_ref, pb_ref, q_ref, u_ref, w_ref,
):
    del s_in, pa_in, pb_in, q_in
    for source, offset in ((low_ref, 0), (high_ref, HALO + ROWS)):
        spectrum(source, HALO, offset, mob_ref, ini_ref, fwd_ref, coef_ref, s_ref, pa_ref, pb_ref, q_ref)

    def apply(k, source, target, join=None, old=None, block=BLOCK, shift=0):
        count = WIDE - 2 * k

        def load(row):
            return [source[row, 8 * m : 8 * m + 8, :] for m in range(6)]

        def body(i, carry):
            above, here = carry
            start = k + i * block
            for e in range(block):
                row = start + e
                below = load(row + 1)
                n = [a + b for a, b in zip(above, below)]
                for h in range(2):
                    t0, t1, t2 = here[h], here[2 + h], here[4 + h]
                    n[h] += roll(t2, 1) + t1
                    n[2 + h] += t0 + t2
                    n[4 + h] += t1 + roll(t0, -1)
                for j in range(3):
                    tile = slice(8 * j, 8 * j + 8)
                    p_a, p_b, q = pa_ref[row, tile, :], pb_ref[row, tile, :], q_ref[row, tile, :]
                    n_a, n_b = n[2 * j], n[2 * j + 1]
                    new = [
                        here[2 * j] + (p_a * n_a - q * n_b),
                        here[2 * j + 1] + (p_b * n_b + q * n_a),
                    ]
                    for h in range(2):
                        m = slice(16 * j + 8 * h, 16 * j + 8 * h + 8)
                        value = new[h]
                        if join is not None:
                            kept = here[2 * j + h] if old is source else old[row, m, :]
                            value = kept + join * value
                        target[row - shift, m, :] = value
                above, here = here, below
            return above, here

        lax.fori_loop(0, -(-count // block), body, (load(k - 1), load(k)))

    apply(1, s_ref, u_ref, 0.2, s_ref)
    k = 1
    for power in (2, 4, 8):
        source = u_ref
        for step in range(power - 1):
            k += 1
            target = (s_ref, w_ref)[step % 2]
            apply(k, source, target)
            source = target
        k += 1
        if power < 8:
            apply(k, source, u_ref, 0.2**power, u_ref)
        else:
            apply(k, source, solved_ref, 0.2**power, u_ref, LAST_BLOCK, FIRST)


WIDE_BUFFER = pltpu.VMEM((PAD, 48, 128), F32)
SOLVED = pltpu.VMEM((KEPT, 48, 128), F32)
HALF_BUFFER = pltpu.VMEM((PAD, 24, 128), F32)


def transform_rows(x, mob, ini, forward, coefs):
    return pl.pallas_call(
        transform_kernel,
        out_shape=(WIDE_BUFFER, HALF_BUFFER, HALF_BUFFER, HALF_BUFFER),
        compiler_params=pltpu.CompilerParams(vmem_limit_bytes=16 * MIB),
        name="transform_rows",
    )(*vmem(x, mob, ini), forward, coefs)


def sweep(low, high, mob, ini, forward, coefs, buffers):
    return pl.pallas_call(
        sweep_kernel,
        out_shape=(SOLVED, WIDE_BUFFER, HALF_BUFFER, HALF_BUFFER, HALF_BUFFER),
        scratch_shapes=[WIDE_BUFFER, WIDE_BUFFER],
        input_output_aliases={6: 1, 7: 2, 8: 3, 9: 4},
        compiler_params=pltpu.CompilerParams(vmem_limit_bytes=24 * MIB),
        name="sweep",
    )(*vmem(low, high, mob, ini), forward, coefs, *vmem(*buffers))[0]


def back_kernel(u_ref, traj_ref, x_ref, mob_ref, inv_ref, out_ref, sums_ref, dir_ref, packed_ref, sem):
    slot = lanes() // 32
    slot16 = lanes(NTM) // 32
    natural = natural_index(NT)
    low_half = lanes(NTM) < 64

    def back(rows):
        y = []
        for row in rows:
            halves = []
            for h in range(2):
                t = [u_ref[row, 16 * k + 8 * h : 16 * k + 8 * h + 8, :] for k in range(3)]
                halves.append(swap_blocks(t + [t[2]], slot, 4))
            y.append(jnp.concatenate([halves[h][g] for g in range(4) for h in range(2)], axis=0))
        values = transform(inv_ref[...], jnp.concatenate(y, axis=1))
        out = []
        for e, row in enumerate(rows):
            v = permute_lanes(values[:, 128 * e : 128 * e + 128], natural)
            dir_ref[row] = v
            out.append(v)
        return out

    back([0, KEPT - 1])

    def back_body(i, _):
        for e, v in enumerate(back([i * BATCH + e + 1 for e in range(BATCH)])):
            for j in range(2):
                both = jnp.where(low_half, v[32 * j : 32 * j + 16], roll(v[32 * j + 16 : 32 * j + 32], 64))
                packed_ref[pl.ds(i * BATCH + e + ROWS * j, NTM, stride=2 * ROWS), :] = both
        return 0

    lax.fori_loop(0, ROWS // BATCH, back_body, 0)
    copy = pltpu.make_async_copy(packed_ref, out_ref, sem)
    copy.start()
    jacobian_sums(dir_ref, traj_ref, x_ref, mob_ref, sums_ref, natural, slot16)
    copy.wait()


def back(u, traj, x, mob, inverse):
    return pl.pallas_call(
        back_kernel,
        in_specs=[pl.BlockSpec(memory_space=pltpu.VMEM)] * 5,
        out_specs=(pl.BlockSpec(memory_space=pltpu.HBM), pl.BlockSpec(memory_space=pltpu.VMEM)),
        out_shape=(pltpu.HBM((NTM * 2 * ROWS, 128), F32), pltpu.VMEM((8, 128), F32)),
        scratch_shapes=[
            pltpu.VMEM((KEPT, NT, 128), F32),
            pltpu.VMEM((NTM * 2 * ROWS, 128), F32),
            pltpu.SemaphoreType.DMA,
        ],
        compiler_params=pltpu.CompilerParams(vmem_limit_bytes=16 * MIB),
        name="back",
    )(*vmem(u, traj, x, mob), inverse)


def jacobian_sums(dir_ref, traj_ref, x_ref, mob_ref, out_ref, natural, slot):
    first_row = lax.broadcasted_iota(jnp.int32, (NTM, 128), 0) == 0

    def own(ref, row):
        slabs = [ref[pl.ds(row + ROWS * j, NTM, stride=2 * ROWS), :] for j in range(2)]
        return jnp.concatenate([roll(slabs[q // 2], 64 * (q % 2)) for q in range(4)], axis=0)

    def fold(values):
        return functools.reduce(jnp.add, [values[8 * i : 8 * i + 8] for i in range(8)])

    def one_row(r):
        v = dir_ref[r + 1]
        neighbours = (dir_ref[r] + dir_ref[r + 2]) + (roll(v, 1) + roll(v, -1))
        carried = jnp.where(first_row, 0.0, pltpu.roll(v[48:64], 1, 0))
        earlier = jnp.concatenate([carried, v[:48]], axis=0)
        mob = mob_ref[pl.ds(r + HALO, 1), :]
        traj = own(traj_ref, r)
        res = jnp.concatenate(halo_tiles(x_ref, r, ROWS, slot), axis=0)
        res = permute_lanes(res, natural)
        reaction = reaction_scale * (3.0 * traj * traj - 1.0)
        applied = (v - earlier) / time_step + mob * (4.0 * v - neighbours) + reaction * v
        return [fold(p) for p in (res * res, res * applied, applied * applied)]

    def body(i, sums):
        parts = [one_row(i * JBATCH + e) for e in range(JBATCH)]
        return tuple(s + functools.reduce(jnp.add, p) for s, p in zip(sums, zip(*parts)))

    zero = jnp.zeros((8, 128), F32)
    sums = lax.fori_loop(0, ROWS // JBATCH, body, (zero, zero, zero))
    totals = [jnp.sum(jnp.where(lanes() < 64, s, 0.0)) for s in sums]
    row = lax.broadcasted_iota(jnp.int32, (8, 128), 0)
    out_ref[...] = jnp.where(row == 0, totals[0], jnp.where(row == 1, totals[1], totals[2]))


def finish_kernel(blocks_ref, sums_ref, out_ref, reduction_ref):
    low_half = lanes() < 64
    norm_square, cross_sum, squared_applied = (
        jnp.broadcast_to(sums_ref[i : i + 1, :], (8, 128)) for i in range(3)
    )
    scale = cross_sum / squared_applied
    first = pl.program_id(0) * PACK_ROWS

    @pl.when(first == 0)
    def _():
        projection = cross_sum / norm_square
        squared_sum = squared_applied / norm_square
        remainder = jnp.maximum(squared_sum - projection * projection, 0.0)
        reduction_ref[...] = jnp.sqrt(remainder / squared_sum)[:1, :1]

    for i in range(0, PACK_ROWS, 8):
        rows = pl.ds(pl.multiple_of(first + i, 8), 8)
        for k in range(8):
            for j in range(2):
                even = blocks_ref[2 * k, j, rows, :] * scale
                odd = blocks_ref[2 * k + 1, j, rows, :] * scale
                lane = slice(128 * k, 128 * k + 128)
                out_ref[2 * j, i : i + 8, lane] = jnp.where(low_half, even, roll(odd, 64))
                out_ref[2 * j + 1, i : i + 8, lane] = jnp.where(low_half, roll(even, 64), odd)


def finish(blocks, sums):
    return pl.pallas_call(
        finish_kernel,
        grid=(ROWS // PACK_ROWS,),
        in_specs=[pl.BlockSpec(memory_space=pltpu.VMEM)] * 2,
        out_specs=(
            pl.BlockSpec((STEPS, PACK_ROWS, COLS), lambda i: (0, i, 0)),
            pl.BlockSpec((1, 1), lambda i: (0, 0)),
        ),
        out_shape=(
            jax.ShapeDtypeStruct((STEPS, ROWS, COLS), F32),
            jax.ShapeDtypeStruct((1, 1), F32),
        ),
        compiler_params=pltpu.CompilerParams(vmem_limit_bytes=8 * MIB),
        name="finish",
    )(*vmem(blocks, sums))


def swap(blocks):
    return lax.all_to_all(blocks, TM, split_axis=0, concat_axis=0, tiled=True)


def shifted(array, axes, size, distance):
    return lax.ppermute(array, axes, [(i, (i + distance) % size) for i in range(size)])


def row_halos(array, dim):
    last = lax.slice_in_dim(array, ROWS - HALO, ROWS, axis=dim)
    first = lax.slice_in_dim(array, 0, HALO, axis=dim)
    return shifted(last, SPACE, NSP, 1), shifted(first, SPACE, NSP, -1)


def own_columns(array):
    block = lax.axis_index(TM)
    padded = jnp.concatenate([array[:, :, -HALO:], array, array[:, :, : HALO + 32]], axis=2)
    return lax.dynamic_slice_in_dim(padded, 64 * block, 128, axis=2)


def by_thirds(field):
    thirds = field[:, :96].reshape(WIDE, 32, 3).transpose(2, 0, 1)
    return jnp.concatenate([thirds] * GROUPS, axis=2)


def around(sums, axis):
    return [shifted(sums, axis, 4, distance) for distance in (1, 2, 3)]


def on_device(trajectory, initial_state, residual, mobility):
    forward, inverse, coefs = time_tables()
    flat = lambda a: a.reshape(-1, 128)
    x = swap(pack(residual, pack_halo_kernel, 3, "pack_halo"))
    fields = own_columns(jnp.stack([mobility, initial_state]))
    below, above = row_halos(fields, 1)
    mob, ini = jnp.concatenate([below, fields, above], axis=1)
    thirds = by_thirds(mob), by_thirds(ini)
    trajectory, thirds = lax.optimization_barrier((trajectory, thirds))
    traj = pack(trajectory, pack_kernel, 2, "pack")
    low, high = row_halos(x, 2)
    buffers = transform_rows(flat(x), *thirds, forward, coefs)
    traj = swap(traj)
    solved = sweep(flat(low), flat(high), *thirds, forward, coefs, buffers)
    packed, sums = back(solved, flat(traj), flat(x), jnp.roll(mob, -HALO, axis=1), inverse)
    sums = sums + shifted(sums, "space_1", 2, 1)
    packed, sums = lax.optimization_barrier((packed, sums))
    blocks = swap(packed.reshape(NTM, 2, ROWS, 128))
    for axis in ("space_0", "tm_1", "tm_0"):
        one, two, three = around(sums, axis)
        sums = (sums + two) + (one + three)
    update, reduction = finish(blocks, sums)
    return update, reduction.reshape(())


def solution(mesh):
    torus = Mesh(mesh.devices.reshape(4, 4, 4, 2), TM + SPACE)
    in_specs = (P(TM, SPACE, None), P(SPACE, None), P(TM, SPACE, None), P(SPACE, None))
    out_specs = (P(TM, SPACE, None), P())
    return jax.shard_map(
        on_device, mesh=torus, in_specs=in_specs, out_specs=out_specs, check_vma=False
    )
```

```python
import functools

import jax
import jax.numpy as jnp
import ml_dtypes
import numpy as np
from jax import lax
from jax.experimental import pallas as pl
from jax.experimental.pallas import tpu as pltpu
from jax.sharding import Mesh
from jax.sharding import PartitionSpec as P

NT = 64
SPACE = ("space_0", "space_1")
TM = ("tm_0", "tm_1")
NTM = 16
NSP = 8
STEPS = NT // NTM
ROWS = 64
COLS = 1024
HALO = 16
WIDE = ROWS + 2 * HALO
PAD = WIDE + 8
FIRST = HALO - 1
KEPT = ROWS + 2
SOLVED_ROWS = 68
PACKED_ROWS = 80
GROUPS = 4
BLOCKS = 2
LAST_BLOCK = 22
BATCH = 4
PACK_ROWS = 32
JBATCH = 4

circ_weight = 0.2
time_step = 0.01
reaction_scale = 40.0

F32 = jnp.float32
BF16 = jnp.bfloat16
MIB = 1024 * 1024


def time_tables():
    steps = np.arange(NT)
    theta = 2.0 * np.pi * np.arange(NT // 2) / NT
    angles = theta[:, None] * steps[None, :]
    forward = np.stack([np.cos(angles), -np.sin(angles)], axis=1).reshape(NT, NT)
    forward[1] = np.cos(np.pi * steps)
    inverse = forward.T * (np.where(steps < 2, 1.0, 2.0) / NT)[None, :]
    factor = circ_weight ** (1.0 / NT)
    shifts = np.repeat((1.0 - factor * np.cos(theta)) / time_step, 2)
    shifts[1] = (1.0 + factor) / time_step
    coupling = np.repeat(-factor * np.sin(theta) / time_step, 2)
    weights = circ_weight ** (steps / NT)
    step_order = np.array([4 * src + q for q in range(4) for src in range(16)])
    coef_order = np.array(
        [2 * (8 * g + p) + half for g in range(GROUPS) for half in range(2) for p in range(8)]
    )
    forward = (forward * weights[None, :])[coef_order][:, step_order]
    inverse = (inverse / weights[:, None])[step_order][:, coef_order]
    by_pair = lambda v: np.repeat(v.reshape(GROUPS, 8).T, 32, axis=1)
    coefs = [by_pair(shifts[0::2]), by_pair(shifts[1::2]), by_pair(coupling[0::2])]
    return split_matrix(forward), split_matrix(inverse), np.stack(coefs).astype(np.float32)


def split_matrix(matrix):
    high = matrix.astype(ml_dtypes.bfloat16)
    low = (matrix - high.astype(np.float64)).astype(ml_dtypes.bfloat16)
    return np.concatenate([np.concatenate([m, m], axis=1) for m in (high, low)], axis=0)


def transform(matrix_ref, count, take, give, stage_ref, result_ref):
    def stage(i):
        for e, values in enumerate(take(i)):
            high = values.astype(BF16)
            stage_ref[:NT, 128 * e : 128 * e + 128] = high
            stage_ref[NT:, 128 * e : 128 * e + 128] = (values - high.astype(F32)).astype(BF16)

    def step(i, _):
        give(jnp.maximum(i - 1, 0), result_ref)
        both = jnp.dot(matrix_ref[...], stage_ref[...], preferred_element_type=F32)
        result_ref[...] = both[:NT] + both[NT:]
        stage(jnp.minimum(i + 1, count - 1))
        return 0

    stage(0)
    lax.fori_loop(0, count + 1, step, 0)


TRANSFORM_SCRATCH = [
    pltpu.VMEM((2 * NT, 128 * BATCH), BF16),
    pltpu.VMEM((NT, 128 * BATCH), F32),
]


def lanes(rows=8):
    return lax.broadcasted_iota(jnp.int32, (rows, 128), 1)


def roll(values, shift):
    shift %= 128
    return values if shift == 0 else pltpu.roll(values, shift, 1)


def permute_lanes(values, index):
    return jnp.take_along_axis(values, index, axis=1, mode="promise_in_bounds")


def pack_kernel(in_ref, out_ref):
    low_half = lanes() < 64
    for rows in (slice(i, i + 8) for i in range(0, PACK_ROWS, 8)):
        for k in range(8):
            for j in range(2):
                lane = slice(128 * k, 128 * k + 128)
                first, second = in_ref[2 * j, rows, lane], in_ref[2 * j + 1, rows, lane]
                out_ref[2 * k, j, rows, :] = jnp.where(low_half, first, roll(second, 64))
                out_ref[2 * k + 1, j, rows, :] = jnp.where(low_half, roll(first, 64), second)


def pack_halo_kernel(in_ref, out_ref):
    lane = lanes()
    slot, q = lane // 32, lane % 32
    for rows in (slice(i, i + 8) for i in range(0, PACK_ROWS, 8)):
        for odd in range(2):
            base = 48 if odd else -16
            index = [(3 * q + jnp.where(slot < 3, slot, j) + base) & 127 for j in range(3)]
            for b in range(odd, NTM, 2):
                k = b // 2
                both = []
                for t in range(4):
                    v = lambda k: in_ref[t, rows, 128 * (k % 8) : 128 * (k % 8) + 128]
                    if odd:
                        both.append(jnp.where(lane < 16, v(k + 1), v(k)))
                    else:
                        both.append(jnp.where(lane < 112, v(k), v(k - 1)))
                for j in range(3):
                    source = permute_lanes(both[j], index[j])
                    out_ref[b, j, rows, :] = jnp.where(
                        slot < 3, source, permute_lanes(both[3], index[j])
                    )


def pack(array, kernel, slabs, name):
    return pl.pallas_call(
        kernel,
        grid=(ROWS // PACK_ROWS,),
        in_specs=[pl.BlockSpec((STEPS, PACK_ROWS, COLS), lambda i: (0, i, 0))],
        out_specs=pl.BlockSpec((NTM, slabs, PACK_ROWS, 128), lambda i: (0, 0, i, 0)),
        out_shape=jax.ShapeDtypeStruct((NTM, slabs, ROWS, 128), F32),
        compiler_params=pltpu.CompilerParams(vmem_limit_bytes=8 * MIB),
        name=name,
    )(array)


def vmem(*arrays):
    return [pltpu.with_memory_space_constraint(a, pltpu.VMEM) for a in arrays]


def halo_tiles(ref, row, rows, slot):
    slabs = [ref[pl.ds(row + rows * j, NTM, stride=3 * rows), :] for j in range(3)]
    last = jnp.where(slot == 0, roll(slabs[0], 32), jnp.where(slot == 1, roll(slabs[1], 64), roll(slabs[2], 96)))
    return slabs + [last]


def swap_blocks(d, slot, count):
    low_half, even = slot < 2, slot % 2 == 0
    d0 = jnp.where(low_half, d[0], roll(d[2], 64))
    d1 = jnp.where(low_half, d[1], roll(d[3], 64))
    d2 = jnp.where(low_half, roll(d[0], 64), d[2])
    d3 = jnp.where(low_half, roll(d[1], 64), d[3])
    out = [
        jnp.where(even, d0, roll(d1, 32)),
        jnp.where(even, roll(d0, -32), d1),
        jnp.where(even, d2, roll(d3, 32)),
    ]
    if count == 4:
        out.append(jnp.where(even, roll(d2, -32), d3))
    return out


def natural_index(rows):
    lane = lanes(rows)
    column = jnp.where(lane < 80, lane + 16, jnp.where(lane < 112, 0, lane - 112))
    return 32 * (column % 3) + column // 3


def spectrum(sources, mob_ref, ini_ref, fwd_ref, coef_ref, s_ref, pa_ref, pb_ref, q_ref, *scratch):
    slot = lanes() // 32
    slot16 = lanes(NTM) // 32
    each = BATCH // len(sources)
    rows = sources[0][1]

    def take(i):
        return [
            jnp.concatenate(halo_tiles(source, i * each + e, rows, slot16), axis=0)
            for source, _, _ in sources
            for e in range(each)
        ]

    def give(i, coefs):
        c = coef_ref[2]
        places = [i * each + e + offset for _, _, offset in sources for e in range(each)]
        for e, row in enumerate(places):
            lane = slice(128 * e, 128 * e + 128)
            parts = [
                swap_blocks(
                    [coefs[16 * g + 8 * h : 16 * g + 8 * h + 8, lane] for g in range(4)], slot, 3
                )
                for h in range(2)
            ]
            for k in range(3):
                mob = jnp.broadcast_to(mob_ref[k, pl.ds(row, 1), :], (8, 128))
                ini = jnp.broadcast_to(ini_ref[k, pl.ds(row, 1), :], (8, 128))
                frozen = reaction_scale * jnp.maximum(3.0 * ini * ini - 1.0, 0.0)
                base = frozen + 4.0 * mob
                diag_a = coef_ref[0] + base
                diag_b = coef_ref[1] + base
                scale = 0.8 / (diag_a * diag_b + c * c)
                k_a, k_b, k_c = diag_b * scale, diag_a * scale, c * scale
                s_a, s_b = parts[0][k], parts[1][k]
                s_ref[row, 16 * k : 16 * k + 8, :] = k_a * s_a - k_c * s_b
                s_ref[row, 16 * k + 8 : 16 * k + 16, :] = k_b * s_b + k_c * s_a
                mob5 = 5.0 * mob
                tile = slice(8 * k, 8 * k + 8)
                pa_ref[row, tile, :] = mob5 * k_a
                pb_ref[row, tile, :] = mob5 * k_b
                q_ref[row, tile, :] = mob5 * k_c

    transform(fwd_ref, rows // each, take, give, *scratch)


def transform_kernel(x_ref, *refs):
    spectrum([(x_ref, ROWS, HALO)], *refs)


def sweep_kernel(
    low_ref, high_ref, mob_ref, ini_ref, fwd_ref, coef_ref, s_in, pa_in, pb_in, q_in,
    solved_ref, s_ref, pa_ref, pb_ref, q_ref, u_ref, w_ref, *scratch,
):
    del s_in, pa_in, pb_in, q_in
    sources = [(low_ref, HALO, 0), (high_ref, HALO, HALO + ROWS)]
    spectrum(sources, mob_ref, ini_ref, fwd_ref, coef_ref, s_ref, pa_ref, pb_ref, q_ref, *scratch)

    def apply(k, source, target, join=None, old=None, shift=0):
        count = WIDE - 2 * k
        block = -(-count // BLOCKS) if shift == 0 else LAST_BLOCK

        def load(row):
            return [source[row, 8 * m : 8 * m + 8, :] for m in range(6)]

        def body(i, carry):
            above, here = carry
            start = k + i * block
            for e in range(block):
                row = start + e
                below = load(row + 1)
                n = [a + b for a, b in zip(above, below)]
                for h in range(2):
                    t0, t1, t2 = here[h], here[2 + h], here[4 + h]
                    n[h] += roll(t2, 1) + t1
                    n[2 + h] += t0 + t2
                    n[4 + h] += t1 + roll(t0, -1)
                for j in range(3):
                    tile = slice(8 * j, 8 * j + 8)
                    p_a, p_b, q = pa_ref[row, tile, :], pb_ref[row, tile, :], q_ref[row, tile, :]
                    n_a, n_b = n[2 * j], n[2 * j + 1]
                    new = [
                        here[2 * j] + (p_a * n_a - q * n_b),
                        here[2 * j + 1] + (p_b * n_b + q * n_a),
                    ]
                    for h in range(2):
                        m = slice(16 * j + 8 * h, 16 * j + 8 * h + 8)
                        value = new[h]
                        if join is not None:
                            kept = here[2 * j + h] if old is source else old[row, m, :]
                            value = kept + join * value
                        target[row - shift, m, :] = value
                above, here = here, below
            return above, here

        lax.fori_loop(0, -(-count // block), body, (load(k - 1), load(k)))

    apply(1, s_ref, u_ref, 0.2, s_ref)
    k = 1
    for power in (2, 4, 8):
        source = u_ref
        for step in range(power - 1):
            k += 1
            target = (s_ref, w_ref)[step % 2]
            apply(k, source, target)
            source = target
        k += 1
        if power < 8:
            apply(k, source, u_ref, 0.2**power, u_ref)
        else:
            apply(k, source, solved_ref, 0.2**power, u_ref, FIRST)


WIDE_BUFFER = pltpu.VMEM((PAD, 48, 128), F32)
SOLVED = pltpu.VMEM((SOLVED_ROWS, 48, 128), F32)
HALF_BUFFER = pltpu.VMEM((PAD, 24, 128), F32)


def transform_rows(x, mob, ini, forward, coefs):
    return pl.pallas_call(
        transform_kernel,
        out_shape=(WIDE_BUFFER, HALF_BUFFER, HALF_BUFFER, HALF_BUFFER),
        scratch_shapes=TRANSFORM_SCRATCH,
        compiler_params=pltpu.CompilerParams(vmem_limit_bytes=16 * MIB),
        name="transform_rows",
    )(*vmem(x, mob, ini), forward, coefs)


def sweep(low, high, mob, ini, forward, coefs, buffers):
    return pl.pallas_call(
        sweep_kernel,
        out_shape=(SOLVED, WIDE_BUFFER, HALF_BUFFER, HALF_BUFFER, HALF_BUFFER),
        scratch_shapes=[WIDE_BUFFER, WIDE_BUFFER, *TRANSFORM_SCRATCH],
        input_output_aliases={6: 1, 7: 2, 8: 3, 9: 4},
        compiler_params=pltpu.CompilerParams(vmem_limit_bytes=24 * MIB),
        name="sweep",
    )(*vmem(low, high, mob, ini), forward, coefs, *vmem(*buffers))[0]


def back_kernel(u_ref, traj_ref, x_ref, mob_ref, inv_ref, out_ref, sums_ref, dir_ref, packed_ref, sem, *scratch):
    slot = lanes() // 32
    slot16 = lanes(NTM) // 32
    natural = natural_index(NT)
    low_half = lanes(NTM) < 64

    flat_ref = packed_ref.reshape(NTM * 2 * PACKED_ROWS, 128)

    def take(i):
        y = []
        for row in (i * BATCH + e for e in range(BATCH)):
            halves = []
            for h in range(2):
                t = [u_ref[row, 16 * k + 8 * h : 16 * k + 8 * h + 8, :] for k in range(3)]
                halves.append(swap_blocks(t + [t[2]], slot, 4))
            y.append(jnp.concatenate([halves[h][g] for g in range(4) for h in range(2)], axis=0))
        return y

    def give(i, result):
        for e in range(BATCH):
            row = i * BATCH + e
            v = permute_lanes(result[:, 128 * e : 128 * e + 128], natural)
            dir_ref[row] = v
            for j in range(2):
                both = jnp.where(low_half, v[32 * j : 32 * j + 16], roll(v[32 * j + 16 : 32 * j + 32], 64))
                flat_ref[pl.ds(row + 7 + PACKED_ROWS * j, NTM, stride=2 * PACKED_ROWS), :] = both

    transform(inv_ref, -(-KEPT // BATCH), take, give, *scratch)
    copy = pltpu.make_async_copy(packed_ref.at[:, pl.ds(8, ROWS), :], out_ref, sem)
    copy.start()
    jacobian_sums(dir_ref, traj_ref, x_ref, mob_ref, sums_ref, natural, slot16)
    copy.wait()


def back(u, traj, x, mob, inverse):
    return pl.pallas_call(
        back_kernel,
        in_specs=[pl.BlockSpec(memory_space=pltpu.VMEM)] * 5,
        out_specs=(pl.BlockSpec(memory_space=pltpu.HBM), pl.BlockSpec(memory_space=pltpu.VMEM)),
        out_shape=(pltpu.HBM((NTM * 2, ROWS, 128), F32), pltpu.VMEM((8, 128), F32)),
        scratch_shapes=[
            pltpu.VMEM((SOLVED_ROWS, NT, 128), F32),
            pltpu.VMEM((NTM * 2, PACKED_ROWS, 128), F32),
            pltpu.SemaphoreType.DMA,
            *TRANSFORM_SCRATCH,
        ],
        compiler_params=pltpu.CompilerParams(vmem_limit_bytes=16 * MIB),
        name="back",
    )(*vmem(u, traj, x, mob), inverse)


def jacobian_sums(dir_ref, traj_ref, x_ref, mob_ref, out_ref, natural, slot):
    first_row = lax.broadcasted_iota(jnp.int32, (NTM, 128), 0) == 0

    def own(ref, row):
        slabs = [ref[pl.ds(row + ROWS * j, NTM, stride=2 * ROWS), :] for j in range(2)]
        return jnp.concatenate([roll(slabs[q // 2], 64 * (q % 2)) for q in range(4)], axis=0)

    def fold(values):
        return functools.reduce(jnp.add, [values[8 * i : 8 * i + 8] for i in range(8)])

    def one_row(r):
        v = dir_ref[r + 1]
        neighbours = (dir_ref[r] + dir_ref[r + 2]) + (roll(v, 1) + roll(v, -1))
        carried = jnp.where(first_row, 0.0, pltpu.roll(v[48:64], 1, 0))
        earlier = jnp.concatenate([carried, v[:48]], axis=0)
        mob = mob_ref[pl.ds(r + HALO, 1), :]
        traj = own(traj_ref, r)
        res = jnp.concatenate(halo_tiles(x_ref, r, ROWS, slot), axis=0)
        res = permute_lanes(res, natural)
        own_factor = (1.0 / time_step - reaction_scale + 4.0 * mob) + (3.0 * reaction_scale) * (traj * traj)
        applied = own_factor * v - (1.0 / time_step) * earlier - mob * neighbours
        return [fold(p) for p in (res * res, res * applied, applied * applied)]

    def body(i, sums):
        parts = [one_row(i * JBATCH + e) for e in range(JBATCH)]
        return tuple(s + functools.reduce(jnp.add, p) for s, p in zip(sums, zip(*parts)))

    zero = jnp.zeros((8, 128), F32)
    sums = lax.fori_loop(0, ROWS // JBATCH, body, (zero, zero, zero))
    totals = [jnp.sum(jnp.where(lanes() < 64, s, 0.0)) for s in sums]
    row = lax.broadcasted_iota(jnp.int32, (8, 128), 0)
    out_ref[...] = jnp.where(row == 0, totals[0], jnp.where(row == 1, totals[1], totals[2]))


def finish_kernel(blocks_ref, sums_ref, out_ref, reduction_ref):
    low_half = lanes() < 64
    norm_square, cross_sum, squared_applied = (
        jnp.broadcast_to(sums_ref[i : i + 1, :], (8, 128)) for i in range(3)
    )
    scale = cross_sum / squared_applied
    first = pl.program_id(0) * PACK_ROWS

    @pl.when(first == 0)
    def _():
        projection = cross_sum / norm_square
        squared_sum = squared_applied / norm_square
        remainder = jnp.maximum(squared_sum - projection * projection, 0.0)
        reduction_ref[...] = jnp.sqrt(remainder / squared_sum)[:1, :1]

    for i in range(0, PACK_ROWS, 8):
        rows = pl.ds(pl.multiple_of(first + i, 8), 8)
        for k in range(8):
            for j in range(2):
                even = blocks_ref[2 * k, j, rows, :] * scale
                odd = blocks_ref[2 * k + 1, j, rows, :] * scale
                lane = slice(128 * k, 128 * k + 128)
                out_ref[2 * j, i : i + 8, lane] = jnp.where(low_half, even, roll(odd, 64))
                out_ref[2 * j + 1, i : i + 8, lane] = jnp.where(low_half, roll(even, 64), odd)


def finish(blocks, sums):
    return pl.pallas_call(
        finish_kernel,
        grid=(ROWS // PACK_ROWS,),
        in_specs=[pl.BlockSpec(memory_space=pltpu.VMEM)] * 2,
        out_specs=(
            pl.BlockSpec((STEPS, PACK_ROWS, COLS), lambda i: (0, i, 0)),
            pl.BlockSpec((1, 1), lambda i: (0, 0)),
        ),
        out_shape=(
            jax.ShapeDtypeStruct((STEPS, ROWS, COLS), F32),
            jax.ShapeDtypeStruct((1, 1), F32),
        ),
        compiler_params=pltpu.CompilerParams(vmem_limit_bytes=8 * MIB),
        name="finish",
    )(*vmem(blocks, sums))


def swap(blocks):
    return lax.all_to_all(blocks, TM, split_axis=0, concat_axis=0, tiled=True)


def shifted(array, axes, size, distance):
    return lax.ppermute(array, axes, [(i, (i + distance) % size) for i in range(size)])


def row_halos(array, dim):
    last = lax.slice_in_dim(array, ROWS - HALO, ROWS, axis=dim)
    first = lax.slice_in_dim(array, 0, HALO, axis=dim)
    return shifted(last, SPACE, NSP, 1), shifted(first, SPACE, NSP, -1)


def own_columns(array):
    block = lax.axis_index(TM)
    padded = jnp.concatenate([array[:, :, -HALO:], array, array[:, :, : HALO + 32]], axis=2)
    return lax.dynamic_slice_in_dim(padded, 64 * block, 128, axis=2)


def by_thirds(field):
    thirds = field[:, :96].reshape(WIDE, 32, 3).transpose(2, 0, 1)
    return jnp.concatenate([thirds] * GROUPS, axis=2)


def around(sums, axis):
    return [shifted(sums, axis, 4, distance) for distance in (1, 2, 3)]


def on_device(trajectory, initial_state, residual, mobility):
    forward, inverse, coefs = time_tables()
    flat = lambda a: a.reshape(-1, 128)
    x = swap(pack(residual, pack_halo_kernel, 3, "pack_halo"))
    fields = own_columns(jnp.stack([mobility, initial_state]))
    below, above = row_halos(fields, 1)
    mob, ini = jnp.concatenate([below, fields, above], axis=1)
    thirds = by_thirds(mob), by_thirds(ini)
    trajectory, thirds = lax.optimization_barrier((trajectory, thirds))
    traj = pack(trajectory, pack_kernel, 2, "pack")
    low, high = row_halos(x, 2)
    buffers = transform_rows(flat(x), *thirds, forward, coefs)
    traj = swap(traj)
    solved = sweep(flat(low), flat(high), *thirds, forward, coefs, buffers)
    packed, sums = back(solved, flat(traj), flat(x), jnp.roll(mob, -HALO, axis=1), inverse)
    sums = sums + shifted(sums, "space_1", 2, 1)
    packed, sums = lax.optimization_barrier((packed, sums))
    blocks = swap(packed.reshape(NTM, 2, ROWS, 128))
    for axis in ("space_0", "tm_1", "tm_0"):
        one, two, three = around(sums, axis)
        sums = (sums + two) + (one + three)
    update, reduction = finish(blocks, sums)
    return update, reduction.reshape(())


def solution(mesh):
    torus = Mesh(mesh.devices.reshape(4, 4, 4, 2), TM + SPACE)
    in_specs = (P(TM, SPACE, None), P(SPACE, None), P(TM, SPACE, None), P(SPACE, None))
    out_specs = (P(TM, SPACE, None), P())
    return jax.shard_map(
        on_device, mesh=torus, in_specs=in_specs, out_specs=out_specs, check_vma=False
    )
```

```python
import functools

import jax
import jax.numpy as jnp
import ml_dtypes
import numpy as np
from jax import lax
from jax.experimental import pallas as pl
from jax.experimental.pallas import tpu as pltpu
from jax.sharding import Mesh
from jax.sharding import PartitionSpec as P

NT = 64
SPACE = ("space_0", "space_1")
TM = ("tm_0", "tm_1")
NTM = 16
NSP = 8
STEPS = NT // NTM
ROWS = 64
COLS = 1024
HALO = 16
WIDE = ROWS + 2 * HALO
PAD = WIDE + 8
FIRST = HALO - 1
KEPT = ROWS + 2
SOLVED_ROWS = 68
PACKED_ROWS = 80
GROUPS = 4
BLOCKS = 1
LAST_BLOCK = 66
BATCH = 4
PACK_ROWS = 32
JBATCH = 4

circ_weight = 0.2
time_step = 0.01
reaction_scale = 40.0

F32 = jnp.float32
BF16 = jnp.bfloat16
MIB = 1024 * 1024


def time_tables():
    steps = np.arange(NT)
    theta = 2.0 * np.pi * np.arange(NT // 2) / NT
    angles = theta[:, None] * steps[None, :]
    forward = np.stack([np.cos(angles), -np.sin(angles)], axis=1).reshape(NT, NT)
    forward[1] = np.cos(np.pi * steps)
    inverse = forward.T * (np.where(steps < 2, 1.0, 2.0) / NT)[None, :]
    factor = circ_weight ** (1.0 / NT)
    shifts = np.repeat((1.0 - factor * np.cos(theta)) / time_step, 2)
    shifts[1] = (1.0 + factor) / time_step
    coupling = np.repeat(-factor * np.sin(theta) / time_step, 2)
    weights = circ_weight ** (steps / NT)
    step_order = np.array([4 * src + q for q in range(4) for src in range(16)])
    coef_order = np.array(
        [2 * (8 * g + p) + half for g in range(GROUPS) for half in range(2) for p in range(8)]
    )
    forward = (forward * weights[None, :])[coef_order][:, step_order]
    inverse = (inverse / weights[:, None])[step_order][:, coef_order]
    by_pair = lambda v: np.repeat(v.reshape(GROUPS, 8).T, 32, axis=1)
    coefs = [by_pair(shifts[0::2]), by_pair(shifts[1::2]), by_pair(coupling[0::2])]
    return split_matrix(forward), split_matrix(inverse), np.stack(coefs).astype(np.float32)


def split_matrix(matrix):
    high = matrix.astype(ml_dtypes.bfloat16)
    low = (matrix - high.astype(np.float64)).astype(ml_dtypes.bfloat16)
    return np.concatenate([np.concatenate([m, m], axis=1) for m in (high, low)], axis=0)


def transform(matrix_ref, count, take, give, stage_ref, result_ref):
    def stage(i):
        for e, values in enumerate(take(i)):
            high = values.astype(BF16)
            stage_ref[:NT, 128 * e : 128 * e + 128] = high
            stage_ref[NT:, 128 * e : 128 * e + 128] = (values - high.astype(F32)).astype(BF16)

    def step(i, _):
        give(jnp.maximum(i - 1, 0), result_ref)
        both = jnp.dot(matrix_ref[...], stage_ref[...], preferred_element_type=F32)
        result_ref[...] = both[:NT] + both[NT:]
        stage(jnp.minimum(i + 1, count - 1))
        return 0

    stage(0)
    lax.fori_loop(0, count + 1, step, 0)


TRANSFORM_SCRATCH = [
    pltpu.VMEM((2 * NT, 128 * BATCH), BF16),
    pltpu.VMEM((NT, 128 * BATCH), F32),
]


def lanes(rows=8):
    return lax.broadcasted_iota(jnp.int32, (rows, 128), 1)


def roll(values, shift):
    shift %= 128
    return values if shift == 0 else pltpu.roll(values, shift, 1)


def permute_lanes(values, index):
    return jnp.take_along_axis(values, index, axis=1, mode="promise_in_bounds")


def pack_kernel(in_ref, out_ref):
    low_half = lanes() < 64
    for rows in (slice(i, i + 8) for i in range(0, PACK_ROWS, 8)):
        for k in range(8):
            for j in range(2):
                lane = slice(128 * k, 128 * k + 128)
                first, second = in_ref[2 * j, rows, lane], in_ref[2 * j + 1, rows, lane]
                out_ref[2 * k, j, rows, :] = jnp.where(low_half, first, roll(second, 64))
                out_ref[2 * k + 1, j, rows, :] = jnp.where(low_half, roll(first, 64), second)


def pack_halo_kernel(in_ref, out_ref):
    lane = lanes()
    slot, q = lane // 32, lane % 32
    for rows in (slice(i, i + 8) for i in range(0, PACK_ROWS, 8)):
        for odd in range(2):
            base = 48 if odd else -16
            index = [(3 * q + jnp.where(slot < 3, slot, j) + base) & 127 for j in range(3)]
            for b in range(odd, NTM, 2):
                k = b // 2
                both = []
                for t in range(4):
                    v = lambda k: in_ref[t, rows, 128 * (k % 8) : 128 * (k % 8) + 128]
                    if odd:
                        both.append(jnp.where(lane < 16, v(k + 1), v(k)))
                    else:
                        both.append(jnp.where(lane < 112, v(k), v(k - 1)))
                for j in range(3):
                    source = permute_lanes(both[j], index[j])
                    out_ref[b, j, rows, :] = jnp.where(
                        slot < 3, source, permute_lanes(both[3], index[j])
                    )


def pack(array, kernel, slabs, name):
    return pl.pallas_call(
        kernel,
        grid=(ROWS // PACK_ROWS,),
        in_specs=[pl.BlockSpec((STEPS, PACK_ROWS, COLS), lambda i: (0, i, 0))],
        out_specs=pl.BlockSpec((NTM, slabs, PACK_ROWS, 128), lambda i: (0, 0, i, 0)),
        out_shape=jax.ShapeDtypeStruct((NTM, slabs, ROWS, 128), F32),
        compiler_params=pltpu.CompilerParams(vmem_limit_bytes=8 * MIB),
        name=name,
    )(array)


def vmem(*arrays):
    return [pltpu.with_memory_space_constraint(a, pltpu.VMEM) for a in arrays]


def halo_tiles(ref, row, rows, slot):
    slabs = [ref[pl.ds(row + rows * j, NTM, stride=3 * rows), :] for j in range(3)]
    last = jnp.where(slot == 0, roll(slabs[0], 32), jnp.where(slot == 1, roll(slabs[1], 64), roll(slabs[2], 96)))
    return slabs + [last]


def swap_blocks(d, slot, count):
    low_half, even = slot < 2, slot % 2 == 0
    d0 = jnp.where(low_half, d[0], roll(d[2], 64))
    d1 = jnp.where(low_half, d[1], roll(d[3], 64))
    d2 = jnp.where(low_half, roll(d[0], 64), d[2])
    d3 = jnp.where(low_half, roll(d[1], 64), d[3])
    out = [
        jnp.where(even, d0, roll(d1, 32)),
        jnp.where(even, roll(d0, -32), d1),
        jnp.where(even, d2, roll(d3, 32)),
    ]
    if count == 4:
        out.append(jnp.where(even, roll(d2, -32), d3))
    return out


def natural_index(rows):
    lane = lanes(rows)
    column = jnp.where(lane < 80, lane + 16, jnp.where(lane < 112, 0, lane - 112))
    return 32 * (column % 3) + column // 3


def spectrum(sources, mob_ref, ini_ref, fwd_ref, coef_ref, s_ref, pa_ref, pb_ref, q_ref, *scratch):
    slot = lanes() // 32
    slot16 = lanes(NTM) // 32
    each = BATCH // len(sources)
    rows = sources[0][1]

    def take(i):
        return [
            jnp.concatenate(halo_tiles(source, i * each + e, rows, slot16), axis=0)
            for source, _, _ in sources
            for e in range(each)
        ]

    def give(i, coefs):
        c = coef_ref[2]
        places = [i * each + e + offset for _, _, offset in sources for e in range(each)]
        for e, row in enumerate(places):
            lane = slice(128 * e, 128 * e + 128)
            parts = [
                swap_blocks(
                    [coefs[16 * g + 8 * h : 16 * g + 8 * h + 8, lane] for g in range(4)], slot, 3
                )
                for h in range(2)
            ]
            for k in range(3):
                mob = jnp.broadcast_to(mob_ref[k, pl.ds(row, 1), :], (8, 128))
                ini = jnp.broadcast_to(ini_ref[k, pl.ds(row, 1), :], (8, 128))
                frozen = reaction_scale * jnp.maximum(3.0 * ini * ini - 1.0, 0.0)
                base = frozen + 4.0 * mob
                diag_a = coef_ref[0] + base
                diag_b = coef_ref[1] + base
                scale = 0.8 / (diag_a * diag_b + c * c)
                k_a, k_b, k_c = diag_b * scale, diag_a * scale, c * scale
                s_a, s_b = parts[0][k], parts[1][k]
                s_ref[row, 16 * k : 16 * k + 8, :] = k_a * s_a - k_c * s_b
                s_ref[row, 16 * k + 8 : 16 * k + 16, :] = k_b * s_b + k_c * s_a
                mob5 = 5.0 * mob
                tile = slice(8 * k, 8 * k + 8)
                pa_ref[row, tile, :] = mob5 * k_a
                pb_ref[row, tile, :] = mob5 * k_b
                q_ref[row, tile, :] = mob5 * k_c

    transform(fwd_ref, rows // each, take, give, *scratch)


def transform_kernel(x_ref, *refs):
    spectrum([(x_ref, ROWS, HALO)], *refs)


def sweep_kernel(
    low_ref, high_ref, mob_ref, ini_ref, fwd_ref, coef_ref, s_in, pa_in, pb_in, q_in,
    solved_ref, s_ref, pa_ref, pb_ref, q_ref, u_ref, w_ref, *scratch,
):
    del s_in, pa_in, pb_in, q_in
    sources = [(low_ref, HALO, 0), (high_ref, HALO, HALO + ROWS)]
    spectrum(sources, mob_ref, ini_ref, fwd_ref, coef_ref, s_ref, pa_ref, pb_ref, q_ref, *scratch)

    def apply(k, source, target, join=None, old=None, shift=0):
        count = WIDE - 2 * k
        block = -(-count // BLOCKS) if shift == 0 else LAST_BLOCK

        def load(row):
            return [source[row, 8 * m : 8 * m + 8, :] for m in range(6)]

        def body(i, carry):
            above, here = carry
            start = k + i * block
            for e in range(block):
                row = start + e
                below = load(row + 1)
                n = [a + b for a, b in zip(above, below)]
                for h in range(2):
                    t0, t1, t2 = here[h], here[2 + h], here[4 + h]
                    n[h] += roll(t2, 1) + t1
                    n[2 + h] += t0 + t2
                    n[4 + h] += t1 + roll(t0, -1)
                for j in range(3):
                    tile = slice(8 * j, 8 * j + 8)
                    p_a, p_b, q = pa_ref[row, tile, :], pb_ref[row, tile, :], q_ref[row, tile, :]
                    n_a, n_b = n[2 * j], n[2 * j + 1]
                    new = [
                        here[2 * j] + (p_a * n_a - q * n_b),
                        here[2 * j + 1] + (p_b * n_b + q * n_a),
                    ]
                    for h in range(2):
                        m = slice(16 * j + 8 * h, 16 * j + 8 * h + 8)
                        value = new[h]
                        if join is not None:
                            kept = here[2 * j + h] if old is source else old[row, m, :]
                            value = kept + join * value
                        target[row - shift, m, :] = value
                above, here = here, below
            return above, here

        lax.fori_loop(0, -(-count // block), body, (load(k - 1), load(k)))

    apply(1, s_ref, u_ref, 0.2, s_ref)
    k = 1
    for power in (2, 4, 8):
        source = u_ref
        for step in range(power - 1):
            k += 1
            target = (s_ref, w_ref)[step % 2]
            apply(k, source, target)
            source = target
        k += 1
        if power < 8:
            apply(k, source, u_ref, 0.2**power, u_ref)
        else:
            apply(k, source, solved_ref, 0.2**power, u_ref, FIRST)


WIDE_BUFFER = pltpu.VMEM((PAD, 48, 128), F32)
SOLVED = pltpu.VMEM((SOLVED_ROWS, 48, 128), F32)
HALF_BUFFER = pltpu.VMEM((PAD, 24, 128), F32)


def transform_rows(x, mob, ini, forward, coefs):
    return pl.pallas_call(
        transform_kernel,
        out_shape=(WIDE_BUFFER, HALF_BUFFER, HALF_BUFFER, HALF_BUFFER),
        scratch_shapes=TRANSFORM_SCRATCH,
        compiler_params=pltpu.CompilerParams(vmem_limit_bytes=16 * MIB),
        name="transform_rows",
    )(*vmem(x, mob, ini), forward, coefs)


def sweep(low, high, mob, ini, forward, coefs, buffers):
    return pl.pallas_call(
        sweep_kernel,
        out_shape=(SOLVED, WIDE_BUFFER, HALF_BUFFER, HALF_BUFFER, HALF_BUFFER),
        scratch_shapes=[WIDE_BUFFER, WIDE_BUFFER, *TRANSFORM_SCRATCH],
        input_output_aliases={6: 1, 7: 2, 8: 3, 9: 4},
        compiler_params=pltpu.CompilerParams(vmem_limit_bytes=24 * MIB),
        name="sweep",
    )(*vmem(low, high, mob, ini), forward, coefs, *vmem(*buffers))[0]


def back_kernel(u_ref, traj_ref, x_ref, mob_ref, inv_ref, out_ref, sums_ref, dir_ref, packed_ref, sem, *scratch):
    slot = lanes() // 32
    slot16 = lanes(NTM) // 32
    natural = natural_index(NT)
    low_half = lanes(NTM) < 64

    flat_ref = packed_ref.reshape(NTM * 2 * PACKED_ROWS, 128)

    def take(i):
        y = []
        for row in (i * BATCH + e for e in range(BATCH)):
            halves = []
            for h in range(2):
                t = [u_ref[row, 16 * k + 8 * h : 16 * k + 8 * h + 8, :] for k in range(3)]
                halves.append(swap_blocks(t + [t[2]], slot, 4))
            y.append(jnp.concatenate([halves[h][g] for g in range(4) for h in range(2)], axis=0))
        return y

    def give(i, result):
        for e in range(BATCH):
            row = i * BATCH + e
            v = permute_lanes(result[:, 128 * e : 128 * e + 128], natural)
            dir_ref[row] = v
            for j in range(2):
                both = jnp.where(low_half, v[32 * j : 32 * j + 16], roll(v[32 * j + 16 : 32 * j + 32], 64))
                flat_ref[pl.ds(row + 7 + PACKED_ROWS * j, NTM, stride=2 * PACKED_ROWS), :] = both

    transform(inv_ref, -(-KEPT // BATCH), take, give, *scratch)
    copy = pltpu.make_async_copy(packed_ref.at[:, pl.ds(8, ROWS), :], out_ref, sem)
    copy.start()
    jacobian_sums(dir_ref, traj_ref, x_ref, mob_ref, sums_ref, natural, slot16)
    copy.wait()


def back(u, traj, x, mob, inverse):
    return pl.pallas_call(
        back_kernel,
        in_specs=[pl.BlockSpec(memory_space=pltpu.VMEM)] * 5,
        out_specs=(pl.BlockSpec(memory_space=pltpu.HBM), pl.BlockSpec(memory_space=pltpu.VMEM)),
        out_shape=(pltpu.HBM((NTM * 2, ROWS, 128), F32), pltpu.VMEM((8, 128), F32)),
        scratch_shapes=[
            pltpu.VMEM((SOLVED_ROWS, NT, 128), F32),
            pltpu.VMEM((NTM * 2, PACKED_ROWS, 128), F32),
            pltpu.SemaphoreType.DMA,
            *TRANSFORM_SCRATCH,
        ],
        compiler_params=pltpu.CompilerParams(vmem_limit_bytes=16 * MIB),
        name="back",
    )(*vmem(u, traj, x, mob), inverse)


def jacobian_sums(dir_ref, traj_ref, x_ref, mob_ref, out_ref, natural, slot):
    first_row = lax.broadcasted_iota(jnp.int32, (NTM, 128), 0) == 0

    def own(ref, row):
        slabs = [ref[pl.ds(row + ROWS * j, NTM, stride=2 * ROWS), :] for j in range(2)]
        return jnp.concatenate([roll(slabs[q // 2], 64 * (q % 2)) for q in range(4)], axis=0)

    def fold(values):
        return functools.reduce(jnp.add, [values[8 * i : 8 * i + 8] for i in range(8)])

    def one_row(r):
        v = dir_ref[r + 1]
        neighbours = (dir_ref[r] + dir_ref[r + 2]) + (roll(v, 1) + roll(v, -1))
        carried = jnp.where(first_row, 0.0, pltpu.roll(v[48:64], 1, 0))
        earlier = jnp.concatenate([carried, v[:48]], axis=0)
        mob = mob_ref[pl.ds(r + HALO, 1), :]
        traj = own(traj_ref, r)
        res = jnp.concatenate(halo_tiles(x_ref, r, ROWS, slot), axis=0)
        res = permute_lanes(res, natural)
        own_factor = (1.0 / time_step - reaction_scale + 4.0 * mob) + (3.0 * reaction_scale) * (traj * traj)
        applied = own_factor * v - (1.0 / time_step) * earlier - mob * neighbours
        return [fold(p) for p in (res * res, res * applied, applied * applied)]

    def body(i, sums):
        parts = [one_row(i * JBATCH + e) for e in range(JBATCH)]
        return tuple(s + functools.reduce(jnp.add, p) for s, p in zip(sums, zip(*parts)))

    zero = jnp.zeros((8, 128), F32)
    sums = lax.fori_loop(0, ROWS // JBATCH, body, (zero, zero, zero))
    totals = [jnp.sum(jnp.where(lanes() < 64, s, 0.0)) for s in sums]
    row = lax.broadcasted_iota(jnp.int32, (8, 128), 0)
    out_ref[...] = jnp.where(row == 0, totals[0], jnp.where(row == 1, totals[1], totals[2]))


def finish_kernel(blocks_ref, sums_ref, out_ref, reduction_ref):
    low_half = lanes() < 64
    norm_square, cross_sum, squared_applied = (
        jnp.broadcast_to(sums_ref[i : i + 1, :], (8, 128)) for i in range(3)
    )
    scale = cross_sum / squared_applied
    first = pl.program_id(0) * PACK_ROWS

    @pl.when(first == 0)
    def _():
        projection = cross_sum / norm_square
        squared_sum = squared_applied / norm_square
        remainder = jnp.maximum(squared_sum - projection * projection, 0.0)
        reduction_ref[...] = jnp.sqrt(remainder / squared_sum)[:1, :1]

    for i in range(0, PACK_ROWS, 8):
        rows = pl.ds(pl.multiple_of(first + i, 8), 8)
        for k in range(8):
            for j in range(2):
                even = blocks_ref[2 * k, j, rows, :] * scale
                odd = blocks_ref[2 * k + 1, j, rows, :] * scale
                lane = slice(128 * k, 128 * k + 128)
                out_ref[2 * j, i : i + 8, lane] = jnp.where(low_half, even, roll(odd, 64))
                out_ref[2 * j + 1, i : i + 8, lane] = jnp.where(low_half, roll(even, 64), odd)


def finish(blocks, sums):
    return pl.pallas_call(
        finish_kernel,
        grid=(ROWS // PACK_ROWS,),
        in_specs=[pl.BlockSpec(memory_space=pltpu.VMEM)] * 2,
        out_specs=(
            pl.BlockSpec((STEPS, PACK_ROWS, COLS), lambda i: (0, i, 0)),
            pl.BlockSpec((1, 1), lambda i: (0, 0)),
        ),
        out_shape=(
            jax.ShapeDtypeStruct((STEPS, ROWS, COLS), F32),
            jax.ShapeDtypeStruct((1, 1), F32),
        ),
        compiler_params=pltpu.CompilerParams(vmem_limit_bytes=8 * MIB),
        name="finish",
    )(*vmem(blocks, sums))


def swap(blocks):
    return lax.all_to_all(blocks, TM, split_axis=0, concat_axis=0, tiled=True)


def shifted(array, axes, size, distance):
    return lax.ppermute(array, axes, [(i, (i + distance) % size) for i in range(size)])


def row_halos(array, dim):
    last = lax.slice_in_dim(array, ROWS - HALO, ROWS, axis=dim)
    first = lax.slice_in_dim(array, 0, HALO, axis=dim)
    return shifted(last, SPACE, NSP, 1), shifted(first, SPACE, NSP, -1)


def own_columns(array):
    block = lax.axis_index(TM)
    padded = jnp.concatenate([array[:, :, -HALO:], array, array[:, :, : HALO + 32]], axis=2)
    return lax.dynamic_slice_in_dim(padded, 64 * block, 128, axis=2)


def by_thirds(field):
    thirds = field[:, :96].reshape(WIDE, 32, 3).transpose(2, 0, 1)
    return jnp.concatenate([thirds] * GROUPS, axis=2)


def around(sums, axis):
    return [shifted(sums, axis, 4, distance) for distance in (1, 2, 3)]


def on_device(trajectory, initial_state, residual, mobility):
    forward, inverse, coefs = time_tables()
    flat = lambda a: a.reshape(-1, 128)
    x = swap(pack(residual, pack_halo_kernel, 3, "pack_halo"))
    fields = own_columns(jnp.stack([mobility, initial_state]))
    below, above = row_halos(fields, 1)
    mob, ini = jnp.concatenate([below, fields, above], axis=1)
    thirds = by_thirds(mob), by_thirds(ini)
    trajectory, thirds = lax.optimization_barrier((trajectory, thirds))
    traj = pack(trajectory, pack_kernel, 2, "pack")
    low, high = row_halos(x, 2)
    buffers = transform_rows(flat(x), *thirds, forward, coefs)
    traj = swap(traj)
    solved = sweep(flat(low), flat(high), *thirds, forward, coefs, buffers)
    packed, sums = back(solved, flat(traj), flat(x), jnp.roll(mob, -HALO, axis=1), inverse)
    sums = sums + shifted(sums, "space_1", 2, 1)
    packed, sums = lax.optimization_barrier((packed, sums))
    blocks = swap(packed.reshape(NTM, 2, ROWS, 128))
    for axis in ("space_0", "tm_1", "tm_0"):
        one, two, three = around(sums, axis)
        sums = (sums + two) + (one + three)
    update, reduction = finish(blocks, sums)
    return update, reduction.reshape(())


def solution(mesh):
    torus = Mesh(mesh.devices.reshape(4, 4, 4, 2), TM + SPACE)
    in_specs = (P(TM, SPACE, None), P(SPACE, None), P(TM, SPACE, None), P(SPACE, None))
    out_specs = (P(TM, SPACE, None), P())
    return jax.shard_map(
        on_device, mesh=torus, in_specs=in_specs, out_specs=out_specs, check_vma=False
    )
```

```python
import functools

import jax
import jax.numpy as jnp
import ml_dtypes
import numpy as np
from jax import lax
from jax.experimental import pallas as pl
from jax.experimental.pallas import tpu as pltpu
from jax.sharding import Mesh
from jax.sharding import PartitionSpec as P

NT = 64
SPACE = ("space_0", "space_1")
TM = ("tm_0", "tm_1")
NTM = 16
NSP = 8
STEPS = NT // NTM
ROWS = 64
COLS = 1024
HALO = 16
WIDE = ROWS + 2 * HALO
PAD = WIDE + 8
FIRST = HALO - 1
KEPT = ROWS + 2
SOLVED_ROWS = 72
PACKED_ROWS = 80
ARRIVING = 3
GROUPS = 4
BLOCKS = 1
LAST_BLOCK = 22
BATCH = 4
PACK_ROWS = 32
JBATCH = 4

circ_weight = 0.2
time_step = 0.01
reaction_scale = 40.0

F32 = jnp.float32
BF16 = jnp.bfloat16
MIB = 1024 * 1024


def time_tables():
    steps = np.arange(NT)
    theta = 2.0 * np.pi * np.arange(NT // 2) / NT
    angles = theta[:, None] * steps[None, :]
    forward = np.stack([np.cos(angles), -np.sin(angles)], axis=1).reshape(NT, NT)
    forward[1] = np.cos(np.pi * steps)
    inverse = forward.T * (np.where(steps < 2, 1.0, 2.0) / NT)[None, :]
    factor = circ_weight ** (1.0 / NT)
    shifts = np.repeat((1.0 - factor * np.cos(theta)) / time_step, 2)
    shifts[1] = (1.0 + factor) / time_step
    coupling = np.repeat(-factor * np.sin(theta) / time_step, 2)
    weights = circ_weight ** (steps / NT)
    step_order = np.array([4 * src + q for q in range(4) for src in range(16)])
    coef_order = np.array(
        [2 * (8 * g + p) + half for g in range(GROUPS) for half in range(2) for p in range(8)]
    )
    forward = (forward * weights[None, :])[coef_order][:, step_order]
    inverse = (inverse / weights[:, None])[step_order][:, coef_order]
    by_pair = lambda v: np.repeat(v.reshape(GROUPS, 8).T, 32, axis=1)
    coefs = [by_pair(shifts[0::2]), by_pair(shifts[1::2]), by_pair(coupling[0::2])]
    return split_matrix(forward), split_matrix(inverse), np.stack(coefs).astype(np.float32)


def split_matrix(matrix):
    high = matrix.astype(ml_dtypes.bfloat16)
    low = (matrix - high.astype(np.float64)).astype(ml_dtypes.bfloat16)
    return np.concatenate([np.concatenate([m, m], axis=1) for m in (high, low)], axis=0)


def transform(matrix_ref, count, take, give, stage_ref, result_ref, ready=lambda i: None):
    def stage(i):
        for e, values in enumerate(take(i)):
            high = values.astype(BF16)
            stage_ref[:NT, 128 * e : 128 * e + 128] = high
            stage_ref[NT:, 128 * e : 128 * e + 128] = (values - high.astype(F32)).astype(BF16)

    def step(i, _):
        ready(i + 1)
        give(jnp.maximum(i - 1, 0), result_ref)
        both = jnp.dot(matrix_ref[...], stage_ref[...], preferred_element_type=F32)
        result_ref[...] = both[:NT] + both[NT:]
        stage(jnp.minimum(i + 1, count - 1))
        return 0

    ready(0)
    stage(0)
    lax.fori_loop(0, count + 1, step, 0)


TRANSFORM_SCRATCH = [
    pltpu.VMEM((2 * NT, 128 * BATCH), BF16),
    pltpu.VMEM((NT, 128 * BATCH), F32),
]


def lanes(rows=8):
    return lax.broadcasted_iota(jnp.int32, (rows, 128), 1)


def roll(values, shift):
    shift %= 128
    return values if shift == 0 else pltpu.roll(values, shift, 1)


def permute_lanes(values, index):
    return jnp.take_along_axis(values, index, axis=1, mode="promise_in_bounds")


def pack_kernel(in_ref, out_ref):
    low_half = lanes() < 64
    for rows in (slice(i, i + 8) for i in range(0, PACK_ROWS, 8)):
        for k in range(8):
            for j in range(2):
                lane = slice(128 * k, 128 * k + 128)
                first, second = in_ref[2 * j, rows, lane], in_ref[2 * j + 1, rows, lane]
                out_ref[2 * k, j, rows, :] = jnp.where(low_half, first, roll(second, 64))
                out_ref[2 * k + 1, j, rows, :] = jnp.where(low_half, roll(first, 64), second)


def pack_halo_kernel(in_ref, out_ref):
    lane = lanes()
    slot, q = lane // 32, lane % 32
    for rows in (slice(i, i + 8) for i in range(0, PACK_ROWS, 8)):
        for odd in range(2):
            base = 48 if odd else -16
            index = [(3 * q + jnp.where(slot < 3, slot, j) + base) & 127 for j in range(3)]
            for b in range(odd, NTM, 2):
                k = b // 2
                both = []
                for t in range(4):
                    v = lambda k: in_ref[t, rows, 128 * (k % 8) : 128 * (k % 8) + 128]
                    if odd:
                        both.append(jnp.where(lane < 16, v(k + 1), v(k)))
                    else:
                        both.append(jnp.where(lane < 112, v(k), v(k - 1)))
                for j in range(3):
                    source = permute_lanes(both[j], index[j])
                    out_ref[b, j, rows, :] = jnp.where(
                        slot < 3, source, permute_lanes(both[3], index[j])
                    )


def pack(array, kernel, slabs, name):
    return pl.pallas_call(
        kernel,
        grid=(ROWS // PACK_ROWS,),
        in_specs=[pl.BlockSpec((STEPS, PACK_ROWS, COLS), lambda i: (0, i, 0))],
        out_specs=pl.BlockSpec((NTM, slabs, PACK_ROWS, 128), lambda i: (0, 0, i, 0)),
        out_shape=jax.ShapeDtypeStruct((NTM, slabs, ROWS, 128), F32),
        compiler_params=pltpu.CompilerParams(vmem_limit_bytes=8 * MIB),
        name=name,
    )(array)


def vmem(*arrays):
    return [pltpu.with_memory_space_constraint(a, pltpu.VMEM) for a in arrays]


def halo_tiles(ref, row, rows, slot):
    slabs = [ref[pl.ds(row + rows * j, NTM, stride=3 * rows), :] for j in range(3)]
    last = jnp.where(slot == 0, roll(slabs[0], 32), jnp.where(slot == 1, roll(slabs[1], 64), roll(slabs[2], 96)))
    return slabs + [last]


def swap_blocks(d, slot, count):
    low_half, even = slot < 2, slot % 2 == 0
    d0 = jnp.where(low_half, d[0], roll(d[2], 64))
    d1 = jnp.where(low_half, d[1], roll(d[3], 64))
    d2 = jnp.where(low_half, roll(d[0], 64), d[2])
    d3 = jnp.where(low_half, roll(d[1], 64), d[3])
    out = [
        jnp.where(even, d0, roll(d1, 32)),
        jnp.where(even, roll(d0, -32), d1),
        jnp.where(even, d2, roll(d3, 32)),
    ]
    if count == 4:
        out.append(jnp.where(even, roll(d2, -32), d3))
    return out


def natural_index(rows):
    lane = lanes(rows)
    column = jnp.where(lane < 80, lane + 16, jnp.where(lane < 112, 0, lane - 112))
    return 32 * (column % 3) + column // 3


def spectrum(sources, mob_ref, ini_ref, fwd_ref, coef_ref, s_ref, pa_ref, pb_ref, q_ref, *scratch):
    slot = lanes() // 32
    slot16 = lanes(NTM) // 32
    each = BATCH // len(sources)
    rows = sources[0][1]

    def take(i):
        return [
            jnp.concatenate(halo_tiles(source, i * each + e, rows, slot16), axis=0)
            for source, _, _ in sources
            for e in range(each)
        ]

    def give(i, coefs):
        c = coef_ref[2]
        places = [i * each + e + offset for _, _, offset in sources for e in range(each)]
        for e, row in enumerate(places):
            lane = slice(128 * e, 128 * e + 128)
            parts = [
                swap_blocks(
                    [coefs[16 * g + 8 * h : 16 * g + 8 * h + 8, lane] for g in range(4)], slot, 3
                )
                for h in range(2)
            ]
            for k in range(3):
                mob = jnp.broadcast_to(mob_ref[k, pl.ds(row, 1), :], (8, 128))
                ini = jnp.broadcast_to(ini_ref[k, pl.ds(row, 1), :], (8, 128))
                frozen = reaction_scale * jnp.maximum(3.0 * ini * ini - 1.0, 0.0)
                base = frozen + 4.0 * mob
                diag_a = coef_ref[0] + base
                diag_b = coef_ref[1] + base
                scale = 0.8 / (diag_a * diag_b + c * c)
                k_a, k_b, k_c = diag_b * scale, diag_a * scale, c * scale
                s_a, s_b = parts[0][k], parts[1][k]
                s_ref[row, 16 * k : 16 * k + 8, :] = k_a * s_a - k_c * s_b
                s_ref[row, 16 * k + 8 : 16 * k + 16, :] = k_b * s_b + k_c * s_a
                mob5 = 5.0 * mob
                tile = slice(8 * k, 8 * k + 8)
                pa_ref[row, tile, :] = mob5 * k_a
                pb_ref[row, tile, :] = mob5 * k_b
                q_ref[row, tile, :] = mob5 * k_c

    transform(fwd_ref, rows // each, take, give, *scratch)


def transform_kernel(x_ref, *refs):
    spectrum([(x_ref, ROWS, HALO)], *refs)


def sweep_kernel(
    low_ref, high_ref, mob_ref, ini_ref, fwd_ref, coef_ref, s_in, pa_in, pb_in, q_in,
    solved_out, s_ref, pa_ref, pb_ref, q_ref, u_ref, w_ref, solved_ref, sems, *scratch,
):
    del s_in, pa_in, pb_in, q_in
    sources = [(low_ref, HALO, 0), (high_ref, HALO, HALO + ROWS)]
    spectrum(sources, mob_ref, ini_ref, fwd_ref, coef_ref, s_ref, pa_ref, pb_ref, q_ref, *scratch)

    def apply(k, source, target, join=None, old=None, shift=0):
        count = WIDE - 2 * k
        block = -(-count // BLOCKS) if shift == 0 else LAST_BLOCK

        def load(row):
            return [source[row, 8 * m : 8 * m + 8, :] for m in range(6)]

        def body(i, carry):
            above, here = carry
            start = k + i * block
            for e in range(block):
                row = start + e
                below = load(row + 1)
                n = [a + b for a, b in zip(above, below)]
                for h in range(2):
                    t0, t1, t2 = here[h], here[2 + h], here[4 + h]
                    n[h] += roll(t2, 1) + t1
                    n[2 + h] += t0 + t2
                    n[4 + h] += t1 + roll(t0, -1)
                for j in range(3):
                    tile = slice(8 * j, 8 * j + 8)
                    p_a, p_b, q = pa_ref[row, tile, :], pb_ref[row, tile, :], q_ref[row, tile, :]
                    n_a, n_b = n[2 * j], n[2 * j + 1]
                    new = [
                        here[2 * j] + (p_a * n_a - q * n_b),
                        here[2 * j + 1] + (p_b * n_b + q * n_a),
                    ]
                    for h in range(2):
                        m = slice(16 * j + 8 * h, 16 * j + 8 * h + 8)
                        value = new[h]
                        if join is not None:
                            kept = here[2 * j + h] if old is source else old[row, m, :]
                            value = kept + join * value
                        target[row - shift, m, :] = value
                above, here = here, below
            if shift:
                solved_copy(i).start()
            return above, here

        lax.fori_loop(0, -(-count // block), body, (load(k - 1), load(k)))

    def solved_copy(i):
        rows = pl.ds(i * LAST_BLOCK, LAST_BLOCK)
        return pltpu.make_async_copy(solved_ref.at[rows], solved_out.at[rows], sems.at[i])

    apply(1, s_ref, u_ref, 0.2, s_ref)
    k = 1
    for power in (2, 4, 8):
        source = u_ref
        for step in range(power - 1):
            k += 1
            target = (s_ref, w_ref)[step % 2]
            apply(k, source, target)
            source = target
        k += 1
        if power < 8:
            apply(k, source, u_ref, 0.2**power, u_ref)
        else:
            apply(k, source, solved_ref, 0.2**power, u_ref, FIRST)
            for i in range(KEPT // LAST_BLOCK):
                solved_copy(i).wait()


WIDE_BUFFER = pltpu.VMEM((PAD, 48, 128), F32)
HALF_BUFFER = pltpu.VMEM((PAD, 24, 128), F32)


def transform_rows(x, mob, ini, forward, coefs):
    return pl.pallas_call(
        transform_kernel,
        out_shape=(WIDE_BUFFER, HALF_BUFFER, HALF_BUFFER, HALF_BUFFER),
        scratch_shapes=TRANSFORM_SCRATCH,
        compiler_params=pltpu.CompilerParams(vmem_limit_bytes=16 * MIB),
        name="transform_rows",
    )(*vmem(x, mob, ini), forward, coefs)


def sweep(low, high, mob, ini, forward, coefs, buffers):
    return pl.pallas_call(
        sweep_kernel,
        in_specs=[pl.BlockSpec(memory_space=pltpu.VMEM)] * 10,
        out_specs=[pl.BlockSpec(memory_space=pltpu.HBM)] + [pl.BlockSpec(memory_space=pltpu.VMEM)] * 4,
        out_shape=(pltpu.HBM((SOLVED_ROWS, 48, 128), F32), WIDE_BUFFER, HALF_BUFFER, HALF_BUFFER, HALF_BUFFER),
        scratch_shapes=[
            WIDE_BUFFER,
            WIDE_BUFFER,
            pltpu.VMEM((KEPT, 48, 128), F32),
            pltpu.SemaphoreType.DMA((KEPT // LAST_BLOCK,)),
            *TRANSFORM_SCRATCH,
        ],
        input_output_aliases={6: 1, 7: 2, 8: 3, 9: 4},
        compiler_params=pltpu.CompilerParams(vmem_limit_bytes=24 * MIB),
        name="sweep",
    )(*vmem(low, high, mob, ini), forward, coefs, *vmem(*buffers))[0]


def back_kernel(
    solved_ref, traj_ref, x_ref, mob_ref, inv_ref, out_ref, sums_ref, dir_ref, packed_ref, sem, u_ref, sems, *scratch
):
    def arriving(i):
        rows = pl.ds(i * ARRIVING * BATCH, ARRIVING * BATCH)
        return pltpu.make_async_copy(solved_ref.at[rows], u_ref.at[rows], sems.at[i])

    for i in range(SOLVED_ROWS // (ARRIVING * BATCH)):
        arriving(i).start()

    def ready(i):
        @pl.when((i % ARRIVING == 0) & (i * BATCH < SOLVED_ROWS))
        def _():
            arriving(i // ARRIVING).wait()

    slot = lanes() // 32
    slot16 = lanes(NTM) // 32
    natural = natural_index(NT)
    low_half = lanes(NTM) < 64

    flat_ref = packed_ref.reshape(NTM * 2 * PACKED_ROWS, 128)

    def take(i):
        y = []
        for row in (i * BATCH + e for e in range(BATCH)):
            halves = []
            for h in range(2):
                t = [u_ref[row, 16 * k + 8 * h : 16 * k + 8 * h + 8, :] for k in range(3)]
                halves.append(swap_blocks(t + [t[2]], slot, 4))
            y.append(jnp.concatenate([halves[h][g] for g in range(4) for h in range(2)], axis=0))
        return y

    def give(i, result):
        for e in range(BATCH):
            row = i * BATCH + e
            v = permute_lanes(result[:, 128 * e : 128 * e + 128], natural)
            dir_ref[row] = v
            for j in range(2):
                both = jnp.where(low_half, v[32 * j : 32 * j + 16], roll(v[32 * j + 16 : 32 * j + 32], 64))
                flat_ref[pl.ds(row + 7 + PACKED_ROWS * j, NTM, stride=2 * PACKED_ROWS), :] = both

    transform(inv_ref, SOLVED_ROWS // BATCH, take, give, *scratch, ready=ready)
    copy = pltpu.make_async_copy(packed_ref.at[:, pl.ds(8, ROWS), :], out_ref, sem)
    copy.start()
    jacobian_sums(dir_ref, traj_ref, x_ref, mob_ref, sums_ref, natural, slot16)
    copy.wait()


def back(solved, traj, x, mob, inverse):
    return pl.pallas_call(
        back_kernel,
        in_specs=[pl.BlockSpec(memory_space=pltpu.HBM)] + [pl.BlockSpec(memory_space=pltpu.VMEM)] * 4,
        out_specs=(pl.BlockSpec(memory_space=pltpu.HBM), pl.BlockSpec(memory_space=pltpu.VMEM)),
        out_shape=(pltpu.HBM((NTM * 2, ROWS, 128), F32), pltpu.VMEM((8, 128), F32)),
        scratch_shapes=[
            pltpu.VMEM((SOLVED_ROWS, NT, 128), F32),
            pltpu.VMEM((NTM * 2, PACKED_ROWS, 128), F32),
            pltpu.SemaphoreType.DMA,
            pltpu.VMEM((SOLVED_ROWS, 48, 128), F32),
            pltpu.SemaphoreType.DMA((SOLVED_ROWS // (ARRIVING * BATCH),)),
            *TRANSFORM_SCRATCH,
        ],
        compiler_params=pltpu.CompilerParams(vmem_limit_bytes=16 * MIB),
        name="back",
    )(pltpu.with_memory_space_constraint(solved, pltpu.HBM), *vmem(traj, x, mob), inverse)


def jacobian_sums(dir_ref, traj_ref, x_ref, mob_ref, out_ref, natural, slot):
    first_row = lax.broadcasted_iota(jnp.int32, (NTM, 128), 0) == 0

    def own(ref, row):
        slabs = [ref[pl.ds(row + ROWS * j, NTM, stride=2 * ROWS), :] for j in range(2)]
        return jnp.concatenate([roll(slabs[q // 2], 64 * (q % 2)) for q in range(4)], axis=0)

    def fold(values):
        return functools.reduce(jnp.add, [values[8 * i : 8 * i + 8] for i in range(8)])

    def one_row(r):
        v = dir_ref[r + 1]
        neighbours = (dir_ref[r] + dir_ref[r + 2]) + (roll(v, 1) + roll(v, -1))
        carried = jnp.where(first_row, 0.0, pltpu.roll(v[48:64], 1, 0))
        earlier = jnp.concatenate([carried, v[:48]], axis=0)
        mob = mob_ref[pl.ds(r + HALO, 1), :]
        traj = own(traj_ref, r)
        res = jnp.concatenate(halo_tiles(x_ref, r, ROWS, slot), axis=0)
        res = permute_lanes(res, natural)
        own_factor = (1.0 / time_step - reaction_scale + 4.0 * mob) + (3.0 * reaction_scale) * (traj * traj)
        applied = own_factor * v - (1.0 / time_step) * earlier - mob * neighbours
        return [fold(p) for p in (res * res, res * applied, applied * applied)]

    def body(i, sums):
        parts = [one_row(i * JBATCH + e) for e in range(JBATCH)]
        return tuple(s + functools.reduce(jnp.add, p) for s, p in zip(sums, zip(*parts)))

    zero = jnp.zeros((8, 128), F32)
    sums = lax.fori_loop(0, ROWS // JBATCH, body, (zero, zero, zero))
    totals = [jnp.sum(jnp.where(lanes() < 64, s, 0.0)) for s in sums]
    row = lax.broadcasted_iota(jnp.int32, (8, 128), 0)
    out_ref[...] = jnp.where(row == 0, totals[0], jnp.where(row == 1, totals[1], totals[2]))


def finish_kernel(blocks_ref, sums_ref, out_ref, reduction_ref):
    low_half = lanes() < 64
    norm_square, cross_sum, squared_applied = (
        jnp.broadcast_to(sums_ref[i : i + 1, :], (8, 128)) for i in range(3)
    )
    scale = cross_sum / squared_applied
    first = pl.program_id(0) * PACK_ROWS

    @pl.when(first == 0)
    def _():
        projection = cross_sum / norm_square
        squared_sum = squared_applied / norm_square
        remainder = jnp.maximum(squared_sum - projection * projection, 0.0)
        reduction_ref[...] = jnp.sqrt(remainder / squared_sum)[:1, :1]

    for i in range(0, PACK_ROWS, 8):
        rows = pl.ds(pl.multiple_of(first + i, 8), 8)
        for k in range(8):
            for j in range(2):
                even = blocks_ref[2 * k, j, rows, :] * scale
                odd = blocks_ref[2 * k + 1, j, rows, :] * scale
                lane = slice(128 * k, 128 * k + 128)
                out_ref[2 * j, i : i + 8, lane] = jnp.where(low_half, even, roll(odd, 64))
                out_ref[2 * j + 1, i : i + 8, lane] = jnp.where(low_half, roll(even, 64), odd)


def finish(blocks, sums):
    return pl.pallas_call(
        finish_kernel,
        grid=(ROWS // PACK_ROWS,),
        in_specs=[pl.BlockSpec(memory_space=pltpu.VMEM)] * 2,
        out_specs=(
            pl.BlockSpec((STEPS, PACK_ROWS, COLS), lambda i: (0, i, 0)),
            pl.BlockSpec((1, 1), lambda i: (0, 0)),
        ),
        out_shape=(
            jax.ShapeDtypeStruct((STEPS, ROWS, COLS), F32),
            jax.ShapeDtypeStruct((1, 1), F32),
        ),
        compiler_params=pltpu.CompilerParams(vmem_limit_bytes=8 * MIB),
        name="finish",
    )(*vmem(blocks, sums))


def swap(blocks):
    return lax.all_to_all(blocks, TM, split_axis=0, concat_axis=0, tiled=True)


def shifted(array, axes, size, distance):
    return lax.ppermute(array, axes, [(i, (i + distance) % size) for i in range(size)])


def row_halos(array, dim):
    last = lax.slice_in_dim(array, ROWS - HALO, ROWS, axis=dim)
    first = lax.slice_in_dim(array, 0, HALO, axis=dim)
    return shifted(last, SPACE, NSP, 1), shifted(first, SPACE, NSP, -1)


def own_columns(array):
    block = lax.axis_index(TM)
    padded = jnp.concatenate([array[:, :, -HALO:], array, array[:, :, : HALO + 32]], axis=2)
    return lax.dynamic_slice_in_dim(padded, 64 * block, 128, axis=2)


def by_thirds(field):
    thirds = field[:, :96].reshape(WIDE, 32, 3).transpose(2, 0, 1)
    return jnp.concatenate([thirds] * GROUPS, axis=2)


def around(sums, axis):
    return [shifted(sums, axis, 4, distance) for distance in (1, 2, 3)]


def on_device(trajectory, initial_state, residual, mobility):
    forward, inverse, coefs = time_tables()
    flat = lambda a: a.reshape(-1, 128)
    x = swap(pack(residual, pack_halo_kernel, 3, "pack_halo"))
    fields = own_columns(jnp.stack([mobility, initial_state]))
    below, above = row_halos(fields, 1)
    mob, ini = jnp.concatenate([below, fields, above], axis=1)
    thirds = by_thirds(mob), by_thirds(ini)
    trajectory, thirds = lax.optimization_barrier((trajectory, thirds))
    traj = pack(trajectory, pack_kernel, 2, "pack")
    low, high = row_halos(x, 2)
    buffers = transform_rows(flat(x), *thirds, forward, coefs)
    traj = swap(traj)
    solved = sweep(flat(low), flat(high), *thirds, forward, coefs, buffers)
    packed, sums = back(solved, flat(traj), flat(x), jnp.roll(mob, -HALO, axis=1), inverse)
    sums = sums + shifted(sums, "space_1", 2, 1)
    packed, sums = lax.optimization_barrier((packed, sums))
    blocks = swap(packed.reshape(NTM, 2, ROWS, 128))
    for axis in ("space_0", "tm_1", "tm_0"):
        one, two, three = around(sums, axis)
        sums = (sums + two) + (one + three)
    update, reduction = finish(blocks, sums)
    return update, reduction.reshape(())


def solution(mesh):
    torus = Mesh(mesh.devices.reshape(4, 4, 4, 2), TM + SPACE)
    in_specs = (P(TM, SPACE, None), P(SPACE, None), P(TM, SPACE, None), P(SPACE, None))
    out_specs = (P(TM, SPACE, None), P())
    return jax.shard_map(
        on_device, mesh=torus, in_specs=in_specs, out_specs=out_specs, check_vma=False
    )
```
